512 devices in a mesh: band: 8 (over y), mem: 64 (over x, z, core).
Axes of the slice: x: 4, y: 8, z: 8, core: 2. Of those that a mesh axis runs over, the one named last changes fastest.
Arguments:
- members: float32 [256, 12, 32768], P('mem', None, 'band'), may hold values from -6 to 6
- diffusivity: float32 [32768], P('band'), may hold values from 0.02 to 0.12
- observed_site: int32 [131072], P(('band', 'mem')), may hold values from 0 to 383
- observed_value: float32 [131072], P(('band', 'mem')), may hold values from -6 to 6
- observed_error: float32 [131072], P(('band', 'mem')), may hold values from 0.5 to 2
- observed_count: int32 [1024], P(('band', 'mem')), may hold values from 1 to 128, 65536 in all
Outputs:
- analysis: float32 [256, 12, 32768], P('mem', None, 'band')
The draws below stay inside these ranges and needn't reach their ends.
Inputs may be any that keep to these rules, and one draw needn't show every extreme that they name: `observed_count`: the counts sum to 65536, and some region has exactly 128.
All inputs are finite; a program needn't handle non-finite values. No bound on the sum of `observed_count` on one device may be relied on, other than what follows from the above.
Results may differ from the reference program's by a relative error of at most 0.00012.
Values sent between devices are 32-bit elements; how exact they have to be, the bound alone decides.
A program may use at most 128 MiB of HBM per device.

```python
import math
import jax
import jax.numpy as jnp
import numpy as np
from jax import lax

SAMPLE_TOTAL = 256
VERTICAL_LAYERS = 4
PROFILE_ENTRIES = 12
NLON = 1024
OBS_DEV = 128
ITERS_NS = 5
NLAT = 32
LATTICE_SITES = 32768
PATCH_PROFILES = 32
STRIP_PATCHES = 128
REGIONS = 1024
NOBS = 131072
N_BAND = 8


def place_ends(entries, rng, least, largest):
    extent = entries.shape
    spot = [jax.random.randint(jax.random.fold_in(rng, axis), (), 0, extent[axis]) for axis in range(len(extent))]
    entries = entries.at[tuple(spot)].set(least)
    longest = extent.index(max(extent))
    spot[longest] = (spot[longest] + 1) % extent[longest]
    return entries.at[tuple(spot)].set(largest)


def steps_of(stream_key, extent, shards, least, high):
    def one(axis_at, parts):
        draws = jax.random.uniform(jax.random.fold_in(jax.random.fold_in(stream_key, 6), axis_at), (parts,), jnp.float32, least / len(shards), high / len(shards))
        return jnp.repeat(jnp.exp(draws), extent[axis_at] // parts).reshape((-1,) + (1,) * (len(extent) - axis_at - 1))

    loudness = one(*shards[0])
    for cut in shards[1:]:
        loudness = loudness * one(*cut)
    return loudness


def length_profile(count, total, limit, lean):
    loads = [(1 << 20) // math.isqrt(grade ** lean) + 1 for grade in range(2, count + 1)]
    spare, holding = total - limit - (count - 1), [1] * (count - 1)
    while spare > 0:
        movable = [i for i in range(count - 1) if holding[i] < limit]
        pool, remaining = sum([loads[i] for i in movable]), spare
        for i in movable:
            addition = min(limit - holding[i], max(1, remaining * loads[i] // pool), spare)
            holding[i] = holding[i] + addition
            spare = spare - addition
    return np.array([limit] + holding)


def ragged(key, number_of, total, most, lean):
    if number_of == 2:
        one = jax.random.randint(key, (), max(1, total - most), min(most, total - 1) + 1)
        return jnp.stack([one, total - one])
    tallies = jnp.asarray(length_profile(number_of, total, most, lean), jnp.int32)
    couples = (number_of - 1) // 2
    donor, sink = tallies[1:1 + 2 * couples:2], tallies[2:2 + 2 * couples:2]
    margin = jnp.minimum(donor - 1, most - sink)
    passed = jax.random.randint(jax.random.fold_in(key, 1), (couples,), 0, 1 << 20) % (margin + 1)
    tallies = tallies.at[1:1 + 2 * couples:2].set(donor - passed).at[2:2 + 2 * couples:2].set(sink + passed)
    return tallies[jax.random.permutation(jax.random.fold_in(key, 2), number_of)]


def bell_draw(stream_key, extent, deviation, bound, shards=(), held_as=jnp.bfloat16):
    factor_of = steps_of(stream_key, extent, shards, -0.22, 0.18) if shards else 1.0
    drawn = jax.random.normal(stream_key, extent, jnp.float32) * deviation * factor_of
    return jnp.minimum(jnp.maximum(drawn, -bound), bound).astype(held_as)


def setup_inputs(seed: int = 0) -> dict:
    seeds = jax.random.split(jax.random.key(seed), 7)
    members = bell_draw(seeds[0], (SAMPLE_TOTAL, PROFILE_ENTRIES, LATTICE_SITES), 1.0, 6.0, ((0, 64), (2, 8)), jnp.float32)
    diffusivity = jnp.clip(jnp.exp(math.log(0.12) - 1.7917595 * jax.random.uniform(seeds[1], (LATTICE_SITES,), jnp.float32) ** steps_of(seeds[1], (LATTICE_SITES,), ((0, 8),), -0.2, 0.2)), 0.02, 0.12)
    observed_site = place_ends(jax.random.randint(seeds[2], (NOBS,), 0, PROFILE_ENTRIES * PATCH_PROFILES), jax.random.fold_in(seeds[2], 1), 0, (PROFILE_ENTRIES * PATCH_PROFILES) - 1).astype(jnp.int32)
    observed_value = bell_draw(seeds[3], (NOBS,), 1.0, 6.0, ((0, 512),), jnp.float32)
    observed_error = jnp.clip(jnp.exp(math.log(2.0) - 1.3862944 * jax.random.uniform(seeds[4], (NOBS,), jnp.float32) ** steps_of(seeds[4], (NOBS,), ((0, 512),), -0.2, 0.2)), 0.5, 2.0)
    observed_count = ragged(seeds[5], REGIONS, REGIONS * OBS_DEV // 2, OBS_DEV, 2).astype(jnp.int32)
    return dict(members=members, diffusivity=diffusivity, observed_site=observed_site, observed_value=observed_value, observed_error=observed_error, observed_count=observed_count)


TRANSPORT_SPEED = 0.5
CORIOLIS = 0.5
PRECISE = lax.Precision.HIGHEST

def evolution_operator(center, upper_neighbour, lower_neighbour, diffusivity, coriolis):
    right_neighbour = jnp.roll(center, -1, axis=3)
    left_neighbour = jnp.roll(center, 1, axis=3)
    laplace = upper_neighbour + lower_neighbour + right_neighbour + left_neighbour - 4.0 * center
    diffused_values = center + diffusivity * laplace
    east_velocity = center[:, VERTICAL_LAYERS:2 * VERTICAL_LAYERS]
    north_velocity = center[:, 2 * VERTICAL_LAYERS:]
    thermal_values = diffused_values[:, :VERTICAL_LAYERS] - 0.5 * TRANSPORT_SPEED * (east_velocity * (right_neighbour[:, :VERTICAL_LAYERS] - left_neighbour[:, :VERTICAL_LAYERS]) + north_velocity * (upper_neighbour[:, :VERTICAL_LAYERS] - lower_neighbour[:, :VERTICAL_LAYERS]))
    updated_east_velocity = diffused_values[:, VERTICAL_LAYERS:2 * VERTICAL_LAYERS] + coriolis * north_velocity
    updated_north_velocity = diffused_values[:, 2 * VERTICAL_LAYERS:] - coriolis * east_velocity
    return jnp.concatenate([thermal_values, updated_east_velocity, updated_north_velocity], axis=1)

def localize(offset, spread):
    return jnp.exp(-0.5 * (offset / spread) ** 2)

def transform_region(gram_matrix, stacked_pert, stacked_weight, stacked_innov, region_flat):
    identity = jnp.eye(gram_matrix.shape[0], dtype=jnp.float32)
    weighted_sum = jnp.dot(stacked_pert, stacked_weight * stacked_innov, precision=PRECISE)
    frobenius = jnp.sqrt(jnp.sum(gram_matrix * gram_matrix))
    iterate = gram_matrix / frobenius
    root_inverse = identity
    for iteration in range(ITERS_NS):
        correction = 1.5 * identity - 0.5 * jnp.dot(root_inverse, iterate, precision=PRECISE)
        iterate = jnp.dot(iterate, correction, precision=PRECISE)
        root_inverse = jnp.dot(correction, root_inverse, precision=PRECISE)
    covariance = jnp.dot(root_inverse, root_inverse, precision=PRECISE) / frobenius
    mean_weights = jnp.dot(covariance, weighted_sum, precision=PRECISE)
    members_count = gram_matrix.shape[0]
    transform = jnp.sqrt((members_count - 1.0) / frobenius) * root_inverse + mean_weights[:, None]
    state_mean = lax.optimization_barrier(jnp.mean(region_flat, axis=0))
    deviations = region_flat - state_mean
    return state_mean + jnp.dot(transform.T, deviations, precision=PRECISE)

def analyze(stacked_pert, stacked_weight, stacked_innov, region_flat):
    identity = jnp.eye(SAMPLE_TOTAL, dtype=jnp.float32)
    gram_matrix = (SAMPLE_TOTAL - 1.0) * identity + jnp.dot(stacked_pert * stacked_weight, stacked_pert.T, precision=PRECISE)
    return transform_region(gram_matrix, stacked_pert, stacked_weight, stacked_innov, region_flat)

def from_lower(grid, mesh_axis):
    padded = jnp.pad(grid, [(1, 0) if dim_index == mesh_axis else (0, 0) for dim_index in range(grid.ndim)])
    return lax.slice_in_dim(padded, 0, grid.shape[mesh_axis], axis=mesh_axis)

def from_upper(grid, mesh_axis):
    padded = jnp.pad(grid, [(0, 1) if dim_index == mesh_axis else (0, 0) for dim_index in range(grid.ndim)])
    return lax.slice_in_dim(padded, 1, grid.shape[mesh_axis] + 1, axis=mesh_axis)

def reference(members, diffusivity, observed_site, observed_value, observed_error, observed_count):
    lattice_arranged = members.reshape(SAMPLE_TOTAL, PROFILE_ENTRIES, NLAT, NLON)
    grid_kappa = diffusivity.reshape(NLAT, NLON)
    latitude = jnp.pi * ((jnp.arange(NLAT).astype(jnp.float32) + 0.5) / NLAT - 0.5)
    coriolis = (CORIOLIS * jnp.sin(latitude))[:, None]

    def lone_sample(single):
        padded = jnp.pad(single, ((0, 0), (1, 1), (0, 0)))
        stepped = evolution_operator(single[None], padded[None, :, 2:], padded[None, :, :-2], grid_kappa, coriolis)
        return stepped[0]
    predicted_vector = lax.map(lone_sample, lattice_arranged).reshape(SAMPLE_TOTAL, PROFILE_ENTRIES, LATTICE_SITES)
    patch_for_position = jnp.arange(NOBS, dtype=jnp.int32) // OBS_DEV
    slot_index = jnp.arange(NOBS, dtype=jnp.int32) % OBS_DEV
    entry_number = observed_site // PATCH_PROFILES
    profile_vector = observed_site % PATCH_PROFILES
    sample_measured = predicted_vector[:, entry_number, patch_for_position * PATCH_PROFILES + profile_vector]
    mean_value = lax.optimization_barrier(jnp.mean(sample_measured, axis=0))
    perturbed = sample_measured - mean_value
    innovation = observed_value - mean_value
    present = (slot_index < observed_count[patch_for_position]).astype(jnp.float32)
    inverse_error = present / observed_error
    offset = profile_vector.astype(jnp.float32) + 0.5 - 0.5 * PATCH_PROFILES
    own_weight = inverse_error * localize(offset, PATCH_PROFILES)
    toward_right = inverse_error * localize(offset - PATCH_PROFILES, PATCH_PROFILES)
    toward_left = inverse_error * localize(offset + PATCH_PROFILES, PATCH_PROFILES)
    pert_grid = perturbed.reshape(SAMPLE_TOTAL, N_BAND, STRIP_PATCHES, OBS_DEV)
    stacked_pert = jnp.concatenate([from_lower(pert_grid, 2), pert_grid, from_upper(pert_grid, 2)], axis=3)
    stacked_pert = stacked_pert.transpose(1, 2, 0, 3)
    shape_grid = (N_BAND, STRIP_PATCHES, OBS_DEV)
    stacked_weight = jnp.concatenate([from_lower(toward_right.reshape(shape_grid), 1), own_weight.reshape(shape_grid), from_upper(toward_left.reshape(shape_grid), 1)], axis=2)
    innov_grid = innovation.reshape(shape_grid)
    stacked_innov = jnp.concatenate([from_lower(innov_grid, 1), innov_grid, from_upper(innov_grid, 1)], axis=2)
    patch_lattice = predicted_vector.reshape(SAMPLE_TOTAL, PROFILE_ENTRIES, N_BAND, STRIP_PATCHES, PATCH_PROFILES).transpose(2, 3, 0, 1, 4)
    patch_lattice = patch_lattice.reshape(N_BAND, STRIP_PATCHES, SAMPLE_TOTAL, PROFILE_ENTRIES * PATCH_PROFILES)

    def one_band(packed):
        return lax.map(lambda item: analyze(item[0], item[1], item[2], item[3]), packed)
    updated = lax.map(one_band, (stacked_pert, stacked_weight, stacked_innov, patch_lattice))
    updated = updated.reshape(N_BAND, STRIP_PATCHES, SAMPLE_TOTAL, PROFILE_ENTRIES, PATCH_PROFILES).transpose(2, 3, 0, 1, 4)
    return updated.reshape(SAMPLE_TOTAL, PROFILE_ENTRIES, LATTICE_SITES)
```

```python
import functools
import math

import jax
import jax.numpy as jnp
from jax import lax
from jax.experimental import pallas as pl
from jax.experimental.pallas import tpu as pltpu
from jax.sharding import PartitionSpec as P

SAMPLE_TOTAL = 256
NLON = 1024
NLAT = 32
N_BAND = 8
N_MEM = 64
HALF = N_MEM // 2
ROWS = NLAT // N_BAND
SLOTS = 128
STATE = 384
CELLS = 32
ITERS_NS = 5
TRANSPORT_SPEED = 0.5
CORIOLIS = 0.5
MESH = pl.DeviceIdType.MESH
F32 = jnp.float32
BF16 = jnp.bfloat16


def owner_of(turn):
    return (turn % HALF) * 2 + turn // HALF


def turn_of_pair(pair):
    return (pair + (N_MEM - 16)) % N_MEM


def split(x):
    high = x.astype(BF16)
    return high, (x - high.astype(F32)).astype(BF16)


def product(left, right, transposed=False):
    dims = (((1,), (1,) if transposed else (0,)), ((), ()))
    dot = functools.partial(lax.dot_general, dimension_numbers=dims, preferred_element_type=F32)
    return dot(left[0], right[0]) + (dot(left[0], right[1]) + dot(left[1], right[0]))


def row_coriolis(band, row):
    value = 0.0
    for b in range(N_BAND):
        latitude = math.pi * ((b * ROWS + row + 0.5) / NLAT - 0.5)
        value = jnp.where(band == b, F32(CORIOLIS * math.sin(latitude)), value)
    return value


def stacked(x):
    return jnp.stack([x[:, i * 128 : (i + 1) * 128] for i in range(NLON // 128)])


def lane_of(shape):
    return lax.broadcasted_iota(jnp.int32, shape, len(shape) - 1)


def sublane_of(shape):
    return lax.broadcasted_iota(jnp.int32, shape, len(shape) - 2)


def exchange_halves(x):
    upper = sublane_of(x.shape) >= 4
    odd = lane_of(x.shape) % 64 >= 32
    other = pltpu.roll(x, 4, axis=1)
    moved = jnp.where(upper, pltpu.roll(other, 96, axis=2), pltpu.roll(other, 32, axis=2))
    return jnp.where(upper == odd, x, moved)


def exchange_blocks(first, second):
    low = lane_of(first.shape) < 64
    return (
        jnp.where(low, first, pltpu.roll(second, 64, axis=2)),
        jnp.where(low, pltpu.roll(first, 64, axis=2), second),
    )


def forecast_row(row, band, state, halo_before, halo_after, kappa, packed):
    here = pl.ds(row * NLON, NLON)
    coriolis = row_coriolis(band, row)
    diffusivity = kappa[:, here]
    fresh = []
    for a in range(2):
        center, north, south, east, west = [], [], [], [], []
        for v in range(3):
            x = state[v, a, :, here]
            center.append(x)
            if row + 1 < ROWS:
                north.append(state[v, a, :, pl.ds((row + 1) * NLON, NLON)])
            else:
                north.append(halo_after[v, a])
            if row > 0:
                south.append(state[v, a, :, pl.ds((row - 1) * NLON, NLON)])
            else:
                south.append(halo_before[v, a])
            east.append(pltpu.roll(x, NLON - 1, axis=1))
            west.append(pltpu.roll(x, 1, axis=1))
        diffused = [
            center[v] + diffusivity * (north[v] + south[v] + east[v] + west[v] - 4.0 * center[v])
            for v in range(3)
        ]
        wind_u, wind_v = center[1], center[2]
        thermal = diffused[0] - 0.5 * TRANSPORT_SPEED * (
            wind_u * (east[0] - west[0]) + wind_v * (north[0] - south[0])
        )
        fresh.append((thermal, diffused[1] + coriolis * wind_v, diffused[2] - coriolis * wind_u))
    base = ((row + 3) % 4) * 8
    for v in range(3):
        pair = exchange_blocks(stacked(fresh[0][v]), stacked(fresh[1][v]))
        for p in range(2):
            packed[pl.ds(base, 8), p, v] = exchange_halves(pair[p])


def unpack_row(row, returned, result):
    base = ((row + 3) % 4) * 8
    for v in range(3):
        pair = [exchange_halves(returned[pl.ds(base, 8), p, v]) for p in range(2)]
        for a, x in enumerate(exchange_blocks(*pair)):
            for i in range(8):
                result[v, a, :, pl.ds(row * NLON + i * 128, 128)] = x[i]


def kernel(
    members,
    kappa,
    site,
    value,
    error,
    count,
    out,
    state,
    halo,
    packed,
    landed,
    reply,
    returned,
    result,
    obs_out,
    obs,
    side_out,
    side_in,
    dev_high,
    dev_low,
    stack_high,
    stack_low,
    load_sem,
    halo_send,
    halo_recv,
    obs_sem,
    fwd_send,
    fwd_recv,
    side_send,
    side_recv,
    back_send,
    back_recv,
    store_sem,
):
    band = lax.axis_index("band")
    me = lax.axis_index("mem")
    core, chip = me % 2, me // 2
    turn = core * HALF + chip
    pair = (turn + 16) % N_MEM

    loads = []
    for c in range(12):
        loads.append(
            pltpu.make_async_copy(
                members.at[c],
                state.at[c // 4, (c // 2) % 2, pl.ds(4 * (c % 2), 4), :],
                load_sem.at[c],
            )
        )
        loads[-1].start()

    barrier = pltpu.get_barrier_semaphore()

    def greet(i, carry):
        pl.semaphore_signal(
            barrier, inc=1, device_id=(band, (me + i) % N_MEM), device_id_type=MESH
        )
        return carry

    lax.fori_loop(1, N_MEM, greet, 0)

    @pl.when(band > 0)
    def _():
        pl.semaphore_signal(barrier, inc=1, device_id=(band - 1, me), device_id_type=MESH)

    @pl.when(band < N_BAND - 1)
    def _():
        pl.semaphore_signal(barrier, inc=1, device_id=(band + 1, me), device_id_type=MESH)

    obs_out[0:2, :] = site[...].astype(F32)
    obs_out[2:4, :] = value[...]
    slot = lax.broadcasted_iota(jnp.int32, (1, SLOTS), 1)
    for q in range(2):
        present = (slot < count[q]).astype(F32)
        obs_out[4 + q : 5 + q, :] = present / error[q : q + 1, :]
    obs_out[6:8, :] = jnp.zeros((2, SLOTS), F32)

    @pl.when(band == 0)
    def _():
        halo[0] = jnp.zeros(halo.shape[1:], F32)

    @pl.when(band == N_BAND - 1)
    def _():
        halo[1] = jnp.zeros(halo.shape[1:], F32)

    for load in loads:
        load.wait()
    for row in (1, 2):
        forecast_row(row, band, state, halo.at[0], halo.at[1], kappa, packed)

    beside = (band > 0).astype(jnp.int32) + (band < N_BAND - 1).astype(jnp.int32)
    pl.semaphore_wait(barrier, N_MEM - 1 + beside)

    up = pltpu.make_async_remote_copy(
        src_ref=state.at[:, :, :, pl.ds((ROWS - 1) * NLON, NLON)],
        dst_ref=halo.at[0],
        send_sem=halo_send.at[0],
        recv_sem=halo_recv.at[0],
        device_id=(jnp.minimum(band + 1, N_BAND - 1), me),
        device_id_type=MESH,
    )
    down = pltpu.make_async_remote_copy(
        src_ref=state.at[:, :, :, pl.ds(0, NLON)],
        dst_ref=halo.at[1],
        send_sem=halo_send.at[1],
        recv_sem=halo_recv.at[1],
        device_id=(jnp.maximum(band - 1, 0), me),
        device_id_type=MESH,
    )

    @pl.when(band < N_BAND - 1)
    def _():
        up.start()

    @pl.when(band > 0)
    def _():
        down.start()

    def dispatch(first):
        def one(i, carry):
            to = (chip + 1 + i) % HALF
            there = first * HALF + to
            target = to * 2 + first

            @pl.when(target != me)
            def _():
                pltpu.make_async_remote_copy(
                    src_ref=packed.at[there // 2, there % 2],
                    dst_ref=landed.at[me],
                    send_sem=fwd_send,
                    recv_sem=fwd_recv,
                    device_id=(band, target),
                    device_id_type=MESH,
                ).start()

            @pl.when(target == me)
            def _():
                pltpu.make_async_copy(
                    packed.at[there // 2, there % 2], landed.at[me], fwd_recv
                ).start()

            return carry

        lax.fori_loop(0, HALF, one, 0)

    dispatch(0)

    obs_owner = owner_of(turn_of_pair(me))
    obs_copy = pltpu.make_async_remote_copy(
        src_ref=obs_out,
        dst_ref=obs,
        send_sem=obs_sem.at[0],
        recv_sem=obs_sem.at[1],
        device_id=(band, obs_owner),
        device_id_type=MESH,
    )

    @pl.when(obs_owner != me)
    def _():
        obs_copy.start()

    @pl.when(obs_owner == me)
    def _():
        pltpu.make_async_copy(obs_out, obs, obs_sem.at[1]).start()

    @pl.when(band > 0)
    def _():
        up.wait_recv()

    @pl.when(band < N_BAND - 1)
    def _():
        down.wait_recv()

    for row in (3, 0):
        forecast_row(row, band, state, halo.at[0], halo.at[1], kappa, packed)
    dispatch(1)

    pltpu.make_async_copy(obs_out, obs, obs_sem.at[1]).wait()
    sites, scales = [], []
    for q in range(2):
        place = obs[q : q + 1, :].astype(jnp.int32)
        sites.append(place)
        offset = (place % CELLS).astype(F32) + 0.5 - 0.5 * CELLS
        inverse = jnp.sqrt(obs[4 + q : 5 + q, :])
        scales.append(
            [
                inverse * jnp.exp(-0.25 * ((offset + shift) / CELLS) ** 2)
                for shift in (0.0, -float(CELLS), float(CELLS))
            ]
        )

    pltpu.make_async_copy(landed, landed, fwd_recv).wait()
    means = [[], []]
    for v in range(3):
        first, second = landed[pl.ds(0, HALF), v], landed[pl.ds(HALF, HALF), v]
        low = sublane_of(first.shape) < 4
        regions = (
            jnp.where(low, first, pltpu.roll(second, 4, axis=1)),
            jnp.where(low, pltpu.roll(first, 4, axis=1), second),
        )
        for q in range(2):
            mean = jnp.sum(jnp.sum(regions[q], axis=0), axis=0, keepdims=True) / SAMPLE_TOTAL
            means[q].append(mean)
            deviation = (regions[q] - mean[None]).reshape(SAMPLE_TOTAL, 128)
            high, small = split(deviation)
            dev_high[q, :, pl.ds(v * 128, 128)] = high
            dev_low[q, :, pl.ds(v * 128, 128)] = small

    lead = lax.broadcasted_iota(jnp.int32, (16, SLOTS), 0) == 0
    means = [jnp.concatenate(m, axis=1) for m in means]
    for q in range(2):
        entry = lax.broadcasted_iota(jnp.int32, (STATE, SLOTS), 0)
        pick = (entry == sites[q]).astype(F32).astype(BF16)
        perturbed = jnp.dot(dev_high[q], pick, preferred_element_type=F32) + jnp.dot(
            dev_low[q], pick, preferred_element_type=F32
        )
        part = lax.broadcasted_iota(jnp.int32, (16, STATE), 0)
        high = means[q].astype(BF16).astype(F32)
        middle = (means[q] - high).astype(BF16).astype(F32)
        small = means[q] - high - middle
        parts = jnp.where(
            part == 0, high, jnp.where(part == 1, middle, jnp.where(part == 2, small, 0.0))
        )
        observed_mean = jnp.sum(
            jnp.dot(parts.astype(BF16), pick, preferred_element_type=F32), axis=0, keepdims=True
        )
        innovation = obs[2 + q : 3 + q, :] - observed_mean
        own, rightward, leftward = scales[q]

        def place_slots(region, column, scale):
            lanes = pl.ds(column * SLOTS, SLOTS)
            high, small = split(perturbed * scale)
            stack_high[region, pl.ds(0, SAMPLE_TOTAL), lanes] = high
            stack_low[region, pl.ds(0, SAMPLE_TOTAL), lanes] = small
            high, small = split(jnp.where(lead, innovation * scale, 0.0))
            stack_high[region, pl.ds(SAMPLE_TOTAL, 16), lanes] = high
            stack_low[region, pl.ds(SAMPLE_TOTAL, 16), lanes] = small

        def side_slots(which, scale):
            side_out[which, pl.ds(0, SAMPLE_TOTAL)] = perturbed * scale
            side_out[which, pl.ds(SAMPLE_TOTAL, 8)] = jnp.where(lead[:8], innovation * scale, 0.0)

        if q == 0:
            side_slots(0, leftward)
        else:
            side_slots(1, rightward)
        place_slots(q, 1, own)
        if q == 0:
            place_slots(1, 0, rightward)
        else:
            place_slots(0, 2, leftward)

    to_left = pltpu.make_async_remote_copy(
        src_ref=side_out.at[0],
        dst_ref=side_in.at[1],
        send_sem=side_send.at[0],
        recv_sem=side_recv.at[1],
        device_id=(band, owner_of(turn_of_pair(jnp.maximum(pair - 1, 0)))),
        device_id_type=MESH,
    )
    to_right = pltpu.make_async_remote_copy(
        src_ref=side_out.at[1],
        dst_ref=side_in.at[0],
        send_sem=side_send.at[1],
        recv_sem=side_recv.at[0],
        device_id=(band, owner_of(turn_of_pair(jnp.minimum(pair + 1, N_MEM - 1)))),
        device_id_type=MESH,
    )

    @pl.when(pair > 0)
    def _():
        to_left.start()

    @pl.when(pair < N_MEM - 1)
    def _():
        to_right.start()

    @pl.when(pair == 0)
    def _():
        side_in[0] = jnp.zeros(side_in.shape[1:], F32)

    @pl.when(pair == N_MEM - 1)
    def _():
        side_in[1] = jnp.zeros(side_in.shape[1:], F32)

    @pl.when(pair > 0)
    def _():
        to_right.wait_recv()

    @pl.when(pair < N_MEM - 1)
    def _():
        to_left.wait_recv()

    for region, column in ((0, 0), (1, 2)):
        lanes = pl.ds(column * SLOTS, SLOTS)
        high, small = split(side_in[region])
        rest = jnp.zeros((8, SLOTS), BF16)
        stack_high[region, pl.ds(0, 272), lanes] = jnp.concatenate([high, rest], axis=0)
        stack_low[region, pl.ds(0, 272), lanes] = jnp.concatenate([small, rest], axis=0)

    shape = (SAMPLE_TOTAL, SAMPLE_TOTAL)
    diagonal = lax.broadcasted_iota(jnp.int32, shape, 0) == lax.broadcasted_iota(
        jnp.int32, shape, 1
    )

    def identity(scale):
        return jnp.where(diagonal, F32(scale), F32(0.0))

    top = lambda x: x[:SAMPLE_TOTAL]
    both = range(2)
    grams = []
    for q in both:
        left = (stack_high[q], stack_low[q])
        grams.append(product(left, (top(left[0]), top(left[1])), transposed=True))
    forces = [g[SAMPLE_TOTAL:] for g in grams]
    grams = [top(g) + identity(SAMPLE_TOTAL - 1.0) for g in grams]
    frobenius = [
        jnp.sqrt(jnp.sum(jnp.sum(g * g, axis=0, keepdims=True), axis=1, keepdims=True))
        for g in grams
    ]
    scaled = [g / f for g, f in zip(grams, frobenius)]
    parts = [split(x) for x in scaled]
    squares = [product(x, x) for x in parts]
    roots = []
    for q in both:
        inner = 0.0625 * squares[q] - 0.5625 * scaled[q] + identity(1.6875)
        roots.append(
            product(split(squares[q]), split(inner)) + identity(2.25) - 2.4375 * scaled[q]
        )
    root_parts = [split(x) for x in roots]
    held = []
    for q in both:
        force = split(forces[q])
        left = tuple(jnp.concatenate([x, f], axis=0) for x, f in zip(parts[q], force))
        held.append(product(left, root_parts[q]))
    forces = [split(x[SAMPLE_TOTAL:]) for x in held]
    held = [split(top(x)) for x in held]
    for iteration in range(2, ITERS_NS):
        last = iteration == ITERS_NS - 1
        corrections = [
            split(identity(1.5) - 0.5 * product(held[q], root_parts[q])) for q in both
        ]
        steps = []
        for q in both:
            pieces = [root_parts[q], forces[q]] if last else [root_parts[q], held[q], forces[q]]
            left = tuple(jnp.concatenate(x, axis=0) for x in zip(*pieces))
            steps.append(product(left, corrections[q]))
        roots = [top(x) for x in steps]
        root_parts = [split(x) for x in roots]
        if not last:
            held = [split(x[SAMPLE_TOTAL : 2 * SAMPLE_TOTAL]) for x in steps]
        forces = [split(x[-16:]) for x in steps]
    updated = []
    for q in both:
        shift = product(forces[q], root_parts[q])[:1] / frobenius[q]
        transform = jnp.sqrt((SAMPLE_TOTAL - 1.0) / frobenius[q]) * roots[q] + shift
        updated.append(product(split(transform), (dev_high[q], dev_low[q])) + means[q])

    for v in range(3):
        first, second = [
            x[:, v * 128 : (v + 1) * 128].reshape(HALF, 8, 128) for x in updated
        ]
        low = sublane_of(first.shape) < 4
        reply[pl.ds(0, HALF), v] = jnp.where(low, first, pltpu.roll(second, 4, axis=1))
        reply[pl.ds(HALF, HALF), v] = jnp.where(low, pltpu.roll(first, 4, axis=1), second)

    def answer(i, carry):
        target = (me + 1 + i) % N_MEM

        @pl.when(target != me)
        def _():
            pltpu.make_async_remote_copy(
                src_ref=reply.at[target],
                dst_ref=returned.at[turn // 2, turn % 2],
                send_sem=back_send,
                recv_sem=back_recv.at[core],
                device_id=(band, target),
                device_id_type=MESH,
            ).start()

        @pl.when(target == me)
        def _():
            pltpu.make_async_copy(
                reply.at[target], returned.at[turn // 2, turn % 2], back_recv.at[core]
            ).start()

        return carry

    lax.fori_loop(0, N_MEM, answer, 0)

    def store(rows, lanes):
        half = returned.at[pl.ds(((rows[0] + 3) % 4) * 8, 16)]
        pltpu.make_async_copy(half, half, back_recv.at[0 if rows[0] == 1 else 1]).wait()
        for row in rows:
            unpack_row(row, returned, result)
        copies = []
        for start, length in lanes:
            for c in range(12):
                copies.append(
                    pltpu.make_async_copy(
                        result.at[
                            c // 4, (c // 2) % 2, pl.ds(4 * (c % 2), 4), pl.ds(start, length)
                        ],
                        out.at[c, :, pl.ds(start, length)],
                        store_sem.at[c, start // NLON],
                    )
                )
                copies[-1].start()
        return copies

    copies = store((1, 2), ((NLON, 2 * NLON),))
    copies += store((3, 0), ((0, NLON), (3 * NLON, NLON)))

    @pl.when(band < N_BAND - 1)
    def _():
        up.wait_send()

    @pl.when(band > 0)
    def _():
        down.wait_send()

    @pl.when(obs_owner != me)
    def _():
        obs_copy.wait_send()

    @pl.when(pair > 0)
    def _():
        to_left.wait_send()

    @pl.when(pair < N_MEM - 1)
    def _():
        to_right.wait_send()

    most = landed.at[pl.ds(0, N_MEM - 1)]
    pltpu.make_async_copy(most, most, fwd_send).wait()
    pltpu.make_async_copy(most, most, back_send).wait()
    for copy in copies:
        copy.wait()


def body(members, diffusivity, observed_site, observed_value, observed_error, observed_count):
    vmem = pl.BlockSpec(memory_space=pltpu.VMEM)
    block = (N_MEM, 3, 8, 128)
    half = (N_MEM // 2, 2, 3, 8, 128)
    state = (3, 2, 8, ROWS * NLON)
    dma = pltpu.SemaphoreType.DMA
    analysis = pl.pallas_call(
        kernel,
        out_shape=jax.ShapeDtypeStruct((12, 4, ROWS * NLON), F32),
        in_specs=[
            pl.BlockSpec(memory_space=pl.ANY),
            vmem,
            vmem,
            vmem,
            vmem,
            pl.BlockSpec(memory_space=pltpu.SMEM),
        ],
        out_specs=pl.BlockSpec(memory_space=pl.ANY),
        scratch_shapes=[
            pltpu.VMEM(state, F32),
            pltpu.VMEM((2, 3, 2, 8, NLON), F32),
            pltpu.VMEM(half, F32),
            pltpu.VMEM(block, F32),
            pltpu.VMEM(block, F32),
            pltpu.VMEM(half, F32),
            pltpu.VMEM(state, F32),
            pltpu.VMEM((8, SLOTS), F32),
            pltpu.VMEM((8, SLOTS), F32),
            pltpu.VMEM((2, 264, SLOTS), F32),
            pltpu.VMEM((2, 264, SLOTS), F32),
            pltpu.VMEM((2, SAMPLE_TOTAL, STATE), BF16),
            pltpu.VMEM((2, SAMPLE_TOTAL, STATE), BF16),
            pltpu.VMEM((2, 272, STATE), BF16),
            pltpu.VMEM((2, 272, STATE), BF16),
            dma((12,)),
            dma((2,)),
            dma((2,)),
            dma((2,)),
            dma,
            dma,
            dma((2,)),
            dma((2,)),
            dma,
            dma((2,)),
            dma((12, 4)),
        ],
        compiler_params=pltpu.CompilerParams(
            collective_id=0, has_side_effects=True, vmem_limit_bytes=56 * 2**20
        ),
    )(
        members.transpose(1, 0, 2),
        diffusivity.reshape(1, ROWS * NLON),
        observed_site.reshape(2, SLOTS),
        observed_value.reshape(2, SLOTS),
        observed_error.reshape(2, SLOTS),
        observed_count,
    )
    return analysis.transpose(1, 0, 2)


def solution(mesh):
    in_specs = (
        P("mem", None, "band"),
        P("band"),
        P(("band", "mem")),
        P(("band", "mem")),
        P(("band", "mem")),
        P(("band", "mem")),
    )
    out_specs = P("mem", None, "band")
    return jax.shard_map(body, mesh=mesh, in_specs=in_specs, out_specs=out_specs, check_vma=False)
```

```python
import functools
import math

import jax
import jax.numpy as jnp
from jax import lax
from jax.experimental import pallas as pl
from jax.experimental.pallas import tpu as pltpu
from jax.sharding import PartitionSpec as P

SAMPLE_TOTAL = 256
NLON = 1024
NLAT = 32
N_BAND = 8
N_MEM = 64
HALF = N_MEM // 2
CHIPS_Z = 8
ROWS = NLAT // N_BAND
SLOTS = 128
STATE = 384
CELLS = 32
TRANSPORT_SPEED = 0.5
CORIOLIS = 0.5
MESH = pl.DeviceIdType.MESH
F32 = jnp.float32
BF16 = jnp.bfloat16


def owner_of(turn):
    return turn % HALF * 2 + turn // HALF


def turn_of_pair(pair):
    return (pair + (N_MEM - 16)) % N_MEM


def split(x):
    high = x.astype(BF16)
    return high, (x - high.astype(F32)).astype(BF16)


def product(left, right, transposed=False):
    dims = (((1,), (1,) if transposed else (0,)), ((), ()))
    dot = functools.partial(lax.dot_general, dimension_numbers=dims, preferred_element_type=F32)
    return dot(left[0], right[0]) + (dot(left[0], right[1]) + dot(left[1], right[0]))


def row_coriolis(band, row):
    value = 0.0
    for b in range(N_BAND):
        latitude = math.pi * ((b * ROWS + row + 0.5) / NLAT - 0.5)
        value = jnp.where(band == b, F32(CORIOLIS * math.sin(latitude)), value)
    return value


def stacked(x):
    return jnp.stack([x[:, i * 128 : (i + 1) * 128] for i in range(NLON // 128)])


def lane_of(shape):
    return lax.broadcasted_iota(jnp.int32, shape, len(shape) - 1)


def sublane_of(shape):
    return lax.broadcasted_iota(jnp.int32, shape, len(shape) - 2)


def exchange_halves(x):
    upper = sublane_of(x.shape) >= 4
    odd = lane_of(x.shape) % 64 >= 32
    other = pltpu.roll(x, 4, axis=1)
    moved = jnp.where(upper, pltpu.roll(other, 96, axis=2), pltpu.roll(other, 32, axis=2))
    return jnp.where(upper == odd, x, moved)


def exchange_blocks(first, second):
    low = lane_of(first.shape) < 64
    return (
        jnp.where(low, first, pltpu.roll(second, 64, axis=2)),
        jnp.where(low, pltpu.roll(first, 64, axis=2), second),
    )


def forecast_row(row, band, state, halo_before, halo_after, kappa, packed):
    here = pl.ds(row * NLON, NLON)
    coriolis = row_coriolis(band, row)
    diffusivity = kappa[:, here]
    fresh = []
    for a in range(2):
        center, north, south, east, west = [], [], [], [], []
        for v in range(3):
            x = state[v, a, :, here]
            center.append(x)
            if row + 1 < ROWS:
                north.append(state[v, a, :, pl.ds((row + 1) * NLON, NLON)])
            else:
                north.append(halo_after[v, a])
            if row > 0:
                south.append(state[v, a, :, pl.ds((row - 1) * NLON, NLON)])
            else:
                south.append(halo_before[v, a])
            east.append(pltpu.roll(x, NLON - 1, axis=1))
            west.append(pltpu.roll(x, 1, axis=1))
        diffused = [
            center[v] + diffusivity * (north[v] + south[v] + east[v] + west[v] - 4.0 * center[v])
            for v in range(3)
        ]
        wind_u, wind_v = center[1], center[2]
        thermal = diffused[0] - 0.5 * TRANSPORT_SPEED * (
            wind_u * (east[0] - west[0]) + wind_v * (north[0] - south[0])
        )
        fresh.append((thermal, diffused[1] + coriolis * wind_v, diffused[2] - coriolis * wind_u))
    base = ((row + 3) % 4) * 8
    for v in range(3):
        pair = exchange_blocks(stacked(fresh[0][v]), stacked(fresh[1][v]))
        for p in range(2):
            packed[pl.ds(base, 8), p, v] = exchange_halves(pair[p])


def unpack_row(row, returned, result):
    base = ((row + 3) % 4) * 8
    for v in range(3):
        pair = [exchange_halves(returned[pl.ds(base, 8), p, v]) for p in range(2)]
        for a, x in enumerate(exchange_blocks(*pair)):
            for i in range(8):
                result[v, a, :, pl.ds(row * NLON + i * 128, 128)] = x[i]


def kernel(
    members,
    kappa,
    site,
    value,
    error,
    count,
    returned,
    state,
    halo,
    packed,
    landed,
    reply,
    obs_out,
    obs,
    side_out,
    side_in,
    dev_high,
    dev_low,
    stack_high,
    stack_low,
    load_sem,
    halo_send,
    halo_recv,
    obs_sem,
    fwd_send,
    fwd_recv,
    side_send,
    side_recv,
    back_send,
    back_recv,
):
    band = lax.axis_index("band")
    me = lax.axis_index("mem")
    turn = me % 2 * HALF + me // 2
    pair = (turn + 16) % N_MEM

    loads = [
        pltpu.make_async_copy(
            members.at[:, :, b], state.at[:, :, pl.ds(4 * b, 4), :], load_sem.at[b]
        )
        for b in range(2)
    ]
    for load in loads:
        load.start()

    barrier = pltpu.get_barrier_semaphore()

    def greet(i, carry):
        pl.semaphore_signal(
            barrier, inc=1, device_id=(band, (me + i) % N_MEM), device_id_type=MESH
        )
        return carry

    lax.fori_loop(1, N_MEM, greet, 0)

    @pl.when(band > 0)
    def _():
        pl.semaphore_signal(barrier, inc=1, device_id=(band - 1, me), device_id_type=MESH)

    @pl.when(band < N_BAND - 1)
    def _():
        pl.semaphore_signal(barrier, inc=1, device_id=(band + 1, me), device_id_type=MESH)

    obs_out[0:2, :] = site[...].astype(F32)
    obs_out[2:4, :] = value[...]
    slot = lax.broadcasted_iota(jnp.int32, (1, SLOTS), 1)
    for q in range(2):
        present = (slot < count[q]).astype(F32)
        obs_out[4 + q : 5 + q, :] = present / error[q : q + 1, :]
    obs_out[6:8, :] = jnp.zeros((2, SLOTS), F32)

    @pl.when(band == 0)
    def _():
        halo[0] = jnp.zeros(halo.shape[1:], F32)

    @pl.when(band == N_BAND - 1)
    def _():
        halo[1] = jnp.zeros(halo.shape[1:], F32)

    for load in loads:
        load.wait()
    forecast_row(1, band, state, halo.at[0], halo.at[1], kappa, packed)

    beside = (band > 0).astype(jnp.int32) + (band < N_BAND - 1).astype(jnp.int32)
    pl.semaphore_wait(barrier, N_MEM - 1 + beside)

    up = pltpu.make_async_remote_copy(
        src_ref=state.at[:, :, :, pl.ds((ROWS - 1) * NLON, NLON)],
        dst_ref=halo.at[0],
        send_sem=halo_send.at[0],
        recv_sem=halo_recv.at[0],
        device_id=(jnp.minimum(band + 1, N_BAND - 1), me),
        device_id_type=MESH,
    )
    down = pltpu.make_async_remote_copy(
        src_ref=state.at[:, :, :, pl.ds(0, NLON)],
        dst_ref=halo.at[1],
        send_sem=halo_send.at[1],
        recv_sem=halo_recv.at[1],
        device_id=(jnp.maximum(band - 1, 0), me),
        device_id_type=MESH,
    )

    @pl.when(band < N_BAND - 1)
    def _():
        up.start()

    @pl.when(band > 0)
    def _():
        down.start()

    def dispatch(q, first, number):
        part = pl.ds(4 * q, 4)

        def send_all(half):
            def one(i, carry):
                there = first + (turn + 1 + i) % number
                target = owner_of(there)
                source = packed.at[there // 2, there % 2, :, part, :]
                place = landed.at[q, :, me % HALF, pl.ds(4 * half, 4), :]

                @pl.when(target != me)
                def _():
                    pltpu.make_async_remote_copy(
                        src_ref=source,
                        dst_ref=place,
                        send_sem=fwd_send,
                        recv_sem=fwd_recv.at[q],
                        device_id=(band, target),
                        device_id_type=MESH,
                    ).start()

                @pl.when(target == me)
                def _():
                    pltpu.make_async_copy(source, place, fwd_recv.at[q]).start()

                return carry

            lax.fori_loop(0, number, one, 0)

        for half in range(2):

            @pl.when(me // HALF == half)
            def _():
                send_all(half)

    forecast_row(2, band, state, halo.at[0], halo.at[1], kappa, packed)
    dispatch(0, 0, 32)
    dispatch(1, 0, 32)

    obs_owner = owner_of(turn_of_pair(me))
    obs_copy = pltpu.make_async_remote_copy(
        src_ref=obs_out,
        dst_ref=obs,
        send_sem=obs_sem.at[0],
        recv_sem=obs_sem.at[1],
        device_id=(band, obs_owner),
        device_id_type=MESH,
    )

    @pl.when(obs_owner != me)
    def _():
        obs_copy.start()

    @pl.when(obs_owner == me)
    def _():
        pltpu.make_async_copy(obs_out, obs, obs_sem.at[1]).start()

    @pl.when(band > 0)
    def _():
        up.wait_recv()

    @pl.when(band < N_BAND - 1)
    def _():
        down.wait_recv()

    for row in (3, 0):
        forecast_row(row, band, state, halo.at[0], halo.at[1], kappa, packed)
    dispatch(0, 32, 32)

    @pl.when(turn >= HALF)
    def _():
        dispatch(1, 32, 32)

    pltpu.make_async_copy(obs_out, obs, obs_sem.at[1]).wait()
    sites, scales = [], []
    for q in range(2):
        spot = obs[q : q + 1, :].astype(jnp.int32)
        sites.append(spot)
        offset = (spot % CELLS).astype(F32) + 0.5 - 0.5 * CELLS
        inverse = jnp.sqrt(obs[4 + q : 5 + q, :])
        scales.append(
            [
                inverse * jnp.exp(-0.25 * ((offset + shift) / CELLS) ** 2)
                for shift in (0.0, -float(CELLS), float(CELLS))
            ]
        )

    to_left = pltpu.make_async_remote_copy(
        src_ref=side_out.at[0],
        dst_ref=side_in.at[1],
        send_sem=side_send.at[0],
        recv_sem=side_recv.at[1],
        device_id=(band, owner_of(turn_of_pair(jnp.maximum(pair - 1, 0)))),
        device_id_type=MESH,
    )
    to_right = pltpu.make_async_remote_copy(
        src_ref=side_out.at[1],
        dst_ref=side_in.at[0],
        send_sem=side_send.at[1],
        recv_sem=side_recv.at[0],
        device_id=(band, owner_of(turn_of_pair(jnp.minimum(pair + 1, N_MEM - 1)))),
        device_id_type=MESH,
    )

    lead = lax.broadcasted_iota(jnp.int32, (16, SLOTS), 0) == 0
    @pl.when(pair == 0)
    def _():
        side_in[0] = jnp.zeros(side_in.shape[1:], F32)

    @pl.when(pair == N_MEM - 1)
    def _():
        side_in[1] = jnp.zeros(side_in.shape[1:], F32)

    means = []
    for q in range(2):
        pltpu.make_async_copy(landed.at[q], landed.at[q], fwd_recv.at[q]).wait()
        mean = []
        for v in range(3):
            region = landed[q, v].reshape(SAMPLE_TOTAL, 128)
            mean.append(jnp.sum(region, axis=0, keepdims=True) / SAMPLE_TOTAL)
            high, small = split(region - mean[-1])
            dev_high[q, :, pl.ds(v * 128, 128)] = high
            dev_low[q, :, pl.ds(v * 128, 128)] = small
        mean = jnp.concatenate(mean, axis=1)
        means.append(mean)
        entry = lax.broadcasted_iota(jnp.int32, (STATE, SLOTS), 0)
        pick = (entry == sites[q]).astype(F32).astype(BF16)
        perturbed = jnp.dot(dev_high[q], pick, preferred_element_type=F32) + jnp.dot(
            dev_low[q], pick, preferred_element_type=F32
        )
        part = lax.broadcasted_iota(jnp.int32, (16, STATE), 0)
        high = mean.astype(BF16).astype(F32)
        middle = (mean - high).astype(BF16).astype(F32)
        small = mean - high - middle
        parts = jnp.where(
            part == 0, high, jnp.where(part == 1, middle, jnp.where(part == 2, small, 0.0))
        )
        observed_mean = jnp.sum(
            jnp.dot(parts.astype(BF16), pick, preferred_element_type=F32), axis=0, keepdims=True
        )
        innovation = obs[2 + q : 3 + q, :] - observed_mean
        own, rightward, leftward = scales[q]

        def place_slots(region, column, scale):
            lanes = pl.ds(column * SLOTS, SLOTS)
            high, small = split(perturbed * scale)
            stack_high[region, pl.ds(0, SAMPLE_TOTAL), lanes] = high
            stack_low[region, pl.ds(0, SAMPLE_TOTAL), lanes] = small
            high, small = split(jnp.where(lead, innovation * scale, 0.0))
            stack_high[region, pl.ds(SAMPLE_TOTAL, 16), lanes] = high
            stack_low[region, pl.ds(SAMPLE_TOTAL, 16), lanes] = small

        def side_slots(which, scale):
            side_out[which, pl.ds(0, SAMPLE_TOTAL)] = perturbed * scale
            side_out[which, pl.ds(SAMPLE_TOTAL, 8)] = jnp.where(lead[:8], innovation * scale, 0.0)

        if q == 0:
            side_slots(0, leftward)

            @pl.when(pair > 0)
            def _():
                to_left.start()

            place_slots(0, 1, own)
            place_slots(1, 0, rightward)
        else:
            side_slots(1, rightward)

            @pl.when(pair < N_MEM - 1)
            def _():
                to_right.start()

            @pl.when(turn < HALF)
            def _():
                dispatch(1, 32, 32)

            place_slots(1, 1, own)
            place_slots(0, 2, leftward)

    shape = (SAMPLE_TOTAL, SAMPLE_TOTAL)
    diagonal = lax.broadcasted_iota(jnp.int32, shape, 0) == lax.broadcasted_iota(
        jnp.int32, shape, 1
    )

    def identity(scale):
        return jnp.where(diagonal, F32(scale), F32(0.0))

    top = lambda x: x[:SAMPLE_TOTAL]

    def two_steps(x, x_parts):
        square = product(x_parts, x_parts)
        inner = 0.0625 * square - 0.5625 * x + identity(1.6875)
        return product(split(square), split(inner)) + identity(2.25) - 2.4375 * x

    def under(*pieces):
        return tuple(jnp.concatenate(x, axis=0) for x in zip(*pieces))

    def analyse(q):
        lanes = pl.ds(2 * q * SLOTS, SLOTS)
        high, small = split(side_in[q])
        rest = jnp.zeros((8, SLOTS), BF16)
        stack_high[q, pl.ds(0, 272), lanes] = jnp.concatenate([high, rest], axis=0)
        stack_low[q, pl.ds(0, 272), lanes] = jnp.concatenate([small, rest], axis=0)

        left = (stack_high[q], stack_low[q])
        gram = product(left, (top(left[0]), top(left[1])), transposed=True)
        force = split(gram[SAMPLE_TOTAL:])
        gram = top(gram) + identity(SAMPLE_TOTAL - 1.0)
        frobenius = jnp.sqrt(
            jnp.sum(jnp.sum(gram * gram, axis=0, keepdims=True), axis=1, keepdims=True)
        )
        scaled = gram / frobenius

        parts = split(scaled)
        root = split(two_steps(scaled, parts))
        held = product(under(parts, force), root)
        force = split(held[SAMPLE_TOTAL:])
        iterate = product(split(top(held)), root)
        parts = split(iterate)
        following = split(two_steps(iterate, parts))
        held = product(under(root, parts, force), following)
        root, force = split(top(held)), split(held[2 * SAMPLE_TOTAL :])
        iterate = product(split(held[SAMPLE_TOTAL : 2 * SAMPLE_TOTAL]), following)
        correction = split(identity(1.5) - 0.5 * iterate)
        held = product(under(root, force), correction)
        force = split(held[SAMPLE_TOTAL:])

        shift = product(force, split(top(held)))[:1] / frobenius
        transform = jnp.sqrt((SAMPLE_TOTAL - 1.0) / frobenius) * top(held) + shift
        updated = product(split(transform), (dev_high[q], dev_low[q])) + means[q]
        for v in range(3):
            reply[q, v] = updated[:, v * 128 : (v + 1) * 128].reshape(HALF, 8, 128)

        def answer(i, carry):
            target = (me + 1 + i) % N_MEM
            place = returned.at[turn // 2, turn % 2, :, pl.ds(4 * q, 4), :]
            for half in range(2):
                source = reply.at[q, :, target % HALF, pl.ds(4 * half, 4), :]

                @pl.when((target != me) & (target // HALF == half))
                def _():
                    pltpu.make_async_remote_copy(
                        src_ref=source,
                        dst_ref=place,
                        send_sem=back_send,
                        recv_sem=back_recv,
                        device_id=(band, target),
                        device_id_type=MESH,
                    ).start()

                @pl.when((target == me) & (target // HALF == half))
                def _():
                    pltpu.make_async_copy(source, place, back_recv).start()

            return carry

        lax.fori_loop(0, N_MEM, answer, 0)

    @pl.when(pair < N_MEM - 1)
    def _():
        to_left.wait_recv()

    analyse(1)

    @pl.when(pair > 0)
    def _():
        to_right.wait_recv()

    analyse(0)

    pltpu.make_async_copy(returned, returned, back_recv).wait()

    @pl.when(band < N_BAND - 1)
    def _():
        up.wait_send()

    @pl.when(band > 0)
    def _():
        down.wait_send()

    @pl.when(obs_owner != me)
    def _():
        obs_copy.wait_send()

    @pl.when(pair > 0)
    def _():
        to_left.wait_send()

    @pl.when(pair < N_MEM - 1)
    def _():
        to_right.wait_send()

    most = returned.at[pl.ds(0, HALF - 1)]
    for sem in (fwd_send, back_send):
        pltpu.make_async_copy(most, most, sem).wait()
        rest = returned.at[HALF - 1, 0]
        pltpu.make_async_copy(rest, rest, sem).wait()


def unpack(arrived, out, returned, result, load_sem, store_sem):
    loads = []
    for row in range(ROWS):
        part = pl.ds((row + 3) % 4 * 8, 8)
        loads.append(
            pltpu.make_async_copy(arrived.at[part], returned.at[part], load_sem.at[row])
        )
        loads[-1].start()
    copies = []
    for row in range(ROWS):
        loads[row].wait()
        unpack_row(row, returned, result)
        lanes = pl.ds(row * NLON, NLON)
        for b in range(2):
            copies.append(
                pltpu.make_async_copy(
                    result.at[:, :, pl.ds(4 * b, 4), lanes],
                    out.at[:, :, b, :, lanes],
                    store_sem.at[b, row],
                )
            )
            copies[-1].start()
    for copy in copies:
        copy.wait()


def body(members, diffusivity, observed_site, observed_value, observed_error, observed_count):
    vmem = pl.BlockSpec(memory_space=pltpu.VMEM)
    block = (2, 3, HALF, 8, 128)
    half = (N_MEM // 2, 2, 3, 8, 128)
    state = (3, 2, 8, ROWS * NLON)
    dma = pltpu.SemaphoreType.DMA
    returned = pl.pallas_call(
        kernel,
        out_shape=jax.ShapeDtypeStruct(half, F32),
        in_specs=[
            pl.BlockSpec(memory_space=pl.ANY),
            vmem,
            vmem,
            vmem,
            vmem,
            pl.BlockSpec(memory_space=pltpu.SMEM),
        ],
        out_specs=pl.BlockSpec(memory_space=pl.ANY),
        scratch_shapes=[
            pltpu.VMEM(state, F32),
            pltpu.VMEM((2, 3, 2, 8, NLON), F32),
            pltpu.VMEM(half, F32),
            pltpu.VMEM(block, F32),
            pltpu.VMEM(block, F32),
            pltpu.VMEM((8, SLOTS), F32),
            pltpu.VMEM((8, SLOTS), F32),
            pltpu.VMEM((2, 264, SLOTS), F32),
            pltpu.VMEM((2, 264, SLOTS), F32),
            pltpu.VMEM((2, SAMPLE_TOTAL, STATE), BF16),
            pltpu.VMEM((2, SAMPLE_TOTAL, STATE), BF16),
            pltpu.VMEM((2, 272, STATE), BF16),
            pltpu.VMEM((2, 272, STATE), BF16),
            dma((2,)),
            dma((2,)),
            dma((2,)),
            dma((2,)),
            dma,
            dma((2,)),
            dma((2,)),
            dma((2,)),
            dma,
            dma,
        ],
        compiler_params=pltpu.CompilerParams(
            collective_id=0, has_side_effects=True, vmem_limit_bytes=60 * 2**20
        ),
    )(
        members.transpose(1, 0, 2).reshape(3, 2, 2, 4, ROWS * NLON),
        diffusivity.reshape(1, ROWS * NLON),
        observed_site.reshape(2, SLOTS),
        observed_value.reshape(2, SLOTS),
        observed_error.reshape(2, SLOTS),
        observed_count,
    )
    analysis = pl.pallas_call(
        unpack,
        out_shape=jax.ShapeDtypeStruct((3, 2, 2, 4, ROWS * NLON), F32),
        in_specs=[pl.BlockSpec(memory_space=pl.ANY)],
        out_specs=pl.BlockSpec(memory_space=pl.ANY),
        scratch_shapes=[
            pltpu.VMEM(half, F32),
            pltpu.VMEM(state, F32),
            dma((ROWS,)),
            dma((2, ROWS)),
        ],
        compiler_params=pltpu.CompilerParams(vmem_limit_bytes=60 * 2**20),
    )(returned)
    return analysis.reshape(12, 4, ROWS * NLON).transpose(1, 0, 2)


def solution(mesh):
    in_specs = (
        P("mem", None, "band"),
        P("band"),
        P(("band", "mem")),
        P(("band", "mem")),
        P(("band", "mem")),
        P(("band", "mem")),
    )
    out_specs = P("mem", None, "band")
    return jax.shard_map(body, mesh=mesh, in_specs=in_specs, out_specs=out_specs, check_vma=False)
```

```python
import functools
import math

import jax
import jax.numpy as jnp
from jax import lax
from jax.experimental import pallas as pl
from jax.experimental.pallas import tpu as pltpu
from jax.sharding import PartitionSpec as P

SAMPLE_TOTAL = 256
NLON = 1024
NLAT = 32
N_BAND = 8
N_MEM = 64
HALF = N_MEM // 2
CHIPS_Z = 8
ROWS = NLAT // N_BAND
SLOTS = 128
STATE = 384
CELLS = 32
TRANSPORT_SPEED = 0.5
CORIOLIS = 0.5
MESH = pl.DeviceIdType.MESH
F32 = jnp.float32
BF16 = jnp.bfloat16


def owner_of(turn):
    return turn % HALF * 2 + turn // HALF


def turn_of_pair(pair):
    return (pair + (N_MEM - 16)) % N_MEM


def split(x):
    high = x.astype(BF16)
    return high, (x - high.astype(F32)).astype(BF16)


def product(left, right, transposed=False):
    dims = (((1,), (1,) if transposed else (0,)), ((), ()))
    dot = functools.partial(lax.dot_general, dimension_numbers=dims, preferred_element_type=F32)
    return dot(left[0], right[0]) + (dot(left[0], right[1]) + dot(left[1], right[0]))


def row_coriolis(band, row):
    value = 0.0
    for b in range(N_BAND):
        latitude = math.pi * ((b * ROWS + row + 0.5) / NLAT - 0.5)
        value = jnp.where(band == b, F32(CORIOLIS * math.sin(latitude)), value)
    return value


def stacked(x):
    return jnp.stack([x[:, i * 128 : (i + 1) * 128] for i in range(NLON // 128)])


def lane_of(shape):
    return lax.broadcasted_iota(jnp.int32, shape, len(shape) - 1)


def sublane_of(shape):
    return lax.broadcasted_iota(jnp.int32, shape, len(shape) - 2)


def exchange_halves(x):
    upper = sublane_of(x.shape) >= 4
    odd = lane_of(x.shape) % 64 >= 32
    other = pltpu.roll(x, 4, axis=1)
    moved = jnp.where(upper, pltpu.roll(other, 96, axis=2), pltpu.roll(other, 32, axis=2))
    return jnp.where(upper == odd, x, moved)


def exchange_blocks(first, second):
    low = lane_of(first.shape) < 64
    return (
        jnp.where(low, first, pltpu.roll(second, 64, axis=2)),
        jnp.where(low, pltpu.roll(first, 64, axis=2), second),
    )


def forecast_row(row, band, state, halo_before, halo_after, kappa, packed):
    here = pl.ds(row * NLON, NLON)
    coriolis = row_coriolis(band, row)
    diffusivity = kappa[:, here]
    fresh = []
    for a in range(2):
        center, north, south, east, west = [], [], [], [], []
        for v in range(3):
            x = state[v, a, :, here]
            center.append(x)
            if row + 1 < ROWS:
                north.append(state[v, a, :, pl.ds((row + 1) * NLON, NLON)])
            else:
                north.append(halo_after[v, a])
            if row > 0:
                south.append(state[v, a, :, pl.ds((row - 1) * NLON, NLON)])
            else:
                south.append(halo_before[v, a])
            east.append(pltpu.roll(x, NLON - 1, axis=1))
            west.append(pltpu.roll(x, 1, axis=1))
        diffused = [
            center[v] + diffusivity * (north[v] + south[v] + east[v] + west[v] - 4.0 * center[v])
            for v in range(3)
        ]
        wind_u, wind_v = center[1], center[2]
        thermal = diffused[0] - 0.5 * TRANSPORT_SPEED * (
            wind_u * (east[0] - west[0]) + wind_v * (north[0] - south[0])
        )
        fresh.append((thermal, diffused[1] + coriolis * wind_v, diffused[2] - coriolis * wind_u))
    base = ((row + 3) % 4) * 8
    for v in range(3):
        pair = exchange_blocks(stacked(fresh[0][v]), stacked(fresh[1][v]))
        for p in range(2):
            packed[pl.ds(base, 8), p, v] = exchange_halves(pair[p])


def unpack_row(row, returned, result):
    base = ((row + 3) % 4) * 8
    for v in range(3):
        pair = [exchange_halves(returned[pl.ds(base, 8), p, v]) for p in range(2)]
        for a, x in enumerate(exchange_blocks(*pair)):
            for i in range(8):
                result[v, a, :, pl.ds(row * NLON + i * 128, 128)] = x[i]


def kernel(
    members,
    kappa,
    site,
    value,
    error,
    count,
    returned,
    state,
    halo,
    packed,
    landed,
    reply,
    obs_out,
    obs,
    side_out,
    side_in,
    dev_high,
    dev_low,
    stack_high,
    stack_low,
    load_sem,
    halo_send,
    halo_recv,
    obs_sem,
    fwd_send,
    fwd_recv,
    side_send,
    side_recv,
    back_send,
    back_recv,
):
    band = lax.axis_index("band")
    me = lax.axis_index("mem")
    turn = me % 2 * HALF + me // 2
    pair = (turn + 16) % N_MEM

    loads = [
        pltpu.make_async_copy(
            members.at[:, :, b], state.at[:, :, pl.ds(4 * b, 4), :], load_sem.at[b]
        )
        for b in range(2)
    ]
    for load in loads:
        load.start()

    barrier = pltpu.get_barrier_semaphore()

    def greet(i, carry):
        pl.semaphore_signal(
            barrier, inc=1, device_id=(band, (me + i) % N_MEM), device_id_type=MESH
        )
        return carry

    lax.fori_loop(1, N_MEM, greet, 0)

    @pl.when(band > 0)
    def _():
        pl.semaphore_signal(barrier, inc=1, device_id=(band - 1, me), device_id_type=MESH)

    @pl.when(band < N_BAND - 1)
    def _():
        pl.semaphore_signal(barrier, inc=1, device_id=(band + 1, me), device_id_type=MESH)

    obs_out[0:2, :] = site[...].astype(F32)
    obs_out[2:4, :] = value[...]
    slot = lax.broadcasted_iota(jnp.int32, (1, SLOTS), 1)
    for q in range(2):
        present = (slot < count[q]).astype(F32)
        obs_out[4 + q : 5 + q, :] = present / error[q : q + 1, :]
    obs_out[6:8, :] = jnp.zeros((2, SLOTS), F32)

    @pl.when(band == 0)
    def _():
        halo[0] = jnp.zeros(halo.shape[1:], F32)

    @pl.when(band == N_BAND - 1)
    def _():
        halo[1] = jnp.zeros(halo.shape[1:], F32)

    for load in loads:
        load.wait()
    forecast_row(1, band, state, halo.at[0], halo.at[1], kappa, packed)

    beside = (band > 0).astype(jnp.int32) + (band < N_BAND - 1).astype(jnp.int32)
    pl.semaphore_wait(barrier, N_MEM - 1 + beside)

    up = pltpu.make_async_remote_copy(
        src_ref=state.at[:, :, :, pl.ds((ROWS - 1) * NLON, NLON)],
        dst_ref=halo.at[0],
        send_sem=halo_send.at[0],
        recv_sem=halo_recv.at[0],
        device_id=(jnp.minimum(band + 1, N_BAND - 1), me),
        device_id_type=MESH,
    )
    down = pltpu.make_async_remote_copy(
        src_ref=state.at[:, :, :, pl.ds(0, NLON)],
        dst_ref=halo.at[1],
        send_sem=halo_send.at[1],
        recv_sem=halo_recv.at[1],
        device_id=(jnp.maximum(band - 1, 0), me),
        device_id_type=MESH,
    )

    @pl.when(band < N_BAND - 1)
    def _():
        up.start()

    @pl.when(band > 0)
    def _():
        down.start()

    def dispatch(q, first, number):
        part = pl.ds(4 * q, 4)

        def send_all(half):
            place = landed.at[q, :, me % HALF, pl.ds(4 * half, 4), :]

            def source(there):
                return packed.at[there // 2, there % 2, :, part, :]

            def send(there):
                pltpu.make_async_remote_copy(
                    src_ref=source(there),
                    dst_ref=place,
                    send_sem=fwd_send,
                    recv_sem=fwd_recv.at[q],
                    device_id=(band, owner_of(there)),
                    device_id_type=MESH,
                ).start()

            def one(i, carry):
                send(first + (turn + 1 + i) % number)
                return carry

            lax.fori_loop(0, number - 1, one, 0)
            last = first + turn % number

            @pl.when(last != turn)
            def _():
                send(last)

            @pl.when(last == turn)
            def _():
                pltpu.make_async_copy(source(turn), place, fwd_recv.at[q]).start()

        for half in range(2):

            @pl.when(me // HALF == half)
            def _():
                send_all(half)

    dispatch(0, 0, 16)
    forecast_row(2, band, state, halo.at[0], halo.at[1], kappa, packed)
    dispatch(0, 16, 16)
    dispatch(1, 0, 32)

    obs_owner = owner_of(turn_of_pair(me))
    obs_copy = pltpu.make_async_remote_copy(
        src_ref=obs_out,
        dst_ref=obs,
        send_sem=obs_sem.at[0],
        recv_sem=obs_sem.at[1],
        device_id=(band, obs_owner),
        device_id_type=MESH,
    )

    @pl.when(obs_owner != me)
    def _():
        obs_copy.start()

    @pl.when(obs_owner == me)
    def _():
        pltpu.make_async_copy(obs_out, obs, obs_sem.at[1]).start()

    @pl.when(band > 0)
    def _():
        up.wait_recv()

    @pl.when(band < N_BAND - 1)
    def _():
        down.wait_recv()

    for row in (3, 0):
        forecast_row(row, band, state, halo.at[0], halo.at[1], kappa, packed)
    dispatch(0, 32, 32)

    @pl.when(turn >= HALF)
    def _():
        dispatch(1, 32, 32)

    pltpu.make_async_copy(obs_out, obs, obs_sem.at[1]).wait()
    sites, scales = [], []
    for q in range(2):
        spot = obs[q : q + 1, :].astype(jnp.int32)
        sites.append(spot)
        offset = (spot % CELLS).astype(F32) + 0.5 - 0.5 * CELLS
        inverse = jnp.sqrt(obs[4 + q : 5 + q, :])
        scales.append(
            [
                inverse * jnp.exp(-0.25 * ((offset + shift) / CELLS) ** 2)
                for shift in (0.0, -float(CELLS), float(CELLS))
            ]
        )

    to_left = pltpu.make_async_remote_copy(
        src_ref=side_out.at[0],
        dst_ref=side_in.at[1],
        send_sem=side_send.at[0],
        recv_sem=side_recv.at[1],
        device_id=(band, owner_of(turn_of_pair(jnp.maximum(pair - 1, 0)))),
        device_id_type=MESH,
    )
    to_right = pltpu.make_async_remote_copy(
        src_ref=side_out.at[1],
        dst_ref=side_in.at[0],
        send_sem=side_send.at[1],
        recv_sem=side_recv.at[0],
        device_id=(band, owner_of(turn_of_pair(jnp.minimum(pair + 1, N_MEM - 1)))),
        device_id_type=MESH,
    )

    lead = lax.broadcasted_iota(jnp.int32, (16, SLOTS), 0) == 0
    @pl.when(pair == 0)
    def _():
        side_in[0] = jnp.zeros(side_in.shape[1:], F32)

    @pl.when(pair == N_MEM - 1)
    def _():
        side_in[1] = jnp.zeros(side_in.shape[1:], F32)

    means = []
    for q in range(2):
        pltpu.make_async_copy(landed.at[q], landed.at[q], fwd_recv.at[q]).wait()
        mean = []
        for v in range(3):
            region = landed[q, v].reshape(SAMPLE_TOTAL, 128)
            mean.append(jnp.sum(region, axis=0, keepdims=True) / SAMPLE_TOTAL)
            high, small = split(region - mean[-1])
            dev_high[q, :, pl.ds(v * 128, 128)] = high
            dev_low[q, :, pl.ds(v * 128, 128)] = small
        mean = jnp.concatenate(mean, axis=1)
        means.append(mean)
        entry = lax.broadcasted_iota(jnp.int32, (STATE, SLOTS), 0)
        pick = (entry == sites[q]).astype(F32).astype(BF16)
        perturbed = jnp.dot(dev_high[q], pick, preferred_element_type=F32) + jnp.dot(
            dev_low[q], pick, preferred_element_type=F32
        )
        part = lax.broadcasted_iota(jnp.int32, (16, STATE), 0)
        high = mean.astype(BF16).astype(F32)
        middle = (mean - high).astype(BF16).astype(F32)
        small = mean - high - middle
        parts = jnp.where(
            part == 0, high, jnp.where(part == 1, middle, jnp.where(part == 2, small, 0.0))
        )
        observed_mean = jnp.sum(
            jnp.dot(parts.astype(BF16), pick, preferred_element_type=F32), axis=0, keepdims=True
        )
        innovation = obs[2 + q : 3 + q, :] - observed_mean
        own, rightward, leftward = scales[q]

        def place_slots(region, column, scale):
            lanes = pl.ds(column * SLOTS, SLOTS)
            high, small = split(perturbed * scale)
            stack_high[region, pl.ds(0, SAMPLE_TOTAL), lanes] = high
            stack_low[region, pl.ds(0, SAMPLE_TOTAL), lanes] = small
            high, small = split(jnp.where(lead, innovation * scale, 0.0))
            stack_high[region, pl.ds(SAMPLE_TOTAL, 16), lanes] = high
            stack_low[region, pl.ds(SAMPLE_TOTAL, 16), lanes] = small

        def side_slots(which, scale):
            side_out[which, pl.ds(0, SAMPLE_TOTAL)] = perturbed * scale
            side_out[which, pl.ds(SAMPLE_TOTAL, 8)] = jnp.where(lead[:8], innovation * scale, 0.0)

        if q == 0:
            side_slots(0, leftward)

            @pl.when(pair > 0)
            def _():
                to_left.start()

            place_slots(0, 1, own)
            place_slots(1, 0, rightward)
        else:
            side_slots(1, rightward)

            @pl.when(pair < N_MEM - 1)
            def _():
                to_right.start()

            @pl.when(turn < HALF)
            def _():
                dispatch(1, 32, 32)

            place_slots(1, 1, own)
            place_slots(0, 2, leftward)

    shape = (SAMPLE_TOTAL, SAMPLE_TOTAL)
    diagonal = lax.broadcasted_iota(jnp.int32, shape, 0) == lax.broadcasted_iota(
        jnp.int32, shape, 1
    )

    def identity(scale):
        return jnp.where(diagonal, F32(scale), F32(0.0))

    top = lambda x: x[:SAMPLE_TOTAL]

    def two_steps(x, x_parts):
        square = product(x_parts, x_parts)
        inner = 0.0625 * square - 0.5625 * x + identity(1.6875)
        return product(split(square), split(inner)) + identity(2.25) - 2.4375 * x

    def under(*pieces):
        return tuple(jnp.concatenate(x, axis=0) for x in zip(*pieces))

    def analyse(q):
        lanes = pl.ds(2 * q * SLOTS, SLOTS)
        high, small = split(side_in[q])
        rest = jnp.zeros((8, SLOTS), BF16)
        stack_high[q, pl.ds(0, 272), lanes] = jnp.concatenate([high, rest], axis=0)
        stack_low[q, pl.ds(0, 272), lanes] = jnp.concatenate([small, rest], axis=0)

        left = (stack_high[q], stack_low[q])
        gram = product(left, (top(left[0]), top(left[1])), transposed=True)
        force = split(gram[SAMPLE_TOTAL:])
        gram = top(gram) + identity(SAMPLE_TOTAL - 1.0)
        frobenius = jnp.sqrt(
            jnp.sum(jnp.sum(gram * gram, axis=0, keepdims=True), axis=1, keepdims=True)
        )
        scaled = gram / frobenius

        parts = split(scaled)
        root = split(two_steps(scaled, parts))
        held = product(under(parts, force), root)
        force = split(held[SAMPLE_TOTAL:])
        iterate = product(split(top(held)), root)
        parts = split(iterate)
        following = split(two_steps(iterate, parts))
        held = product(under(root, parts, force), following)
        root, force = split(top(held)), split(held[2 * SAMPLE_TOTAL :])
        iterate = product(split(held[SAMPLE_TOTAL : 2 * SAMPLE_TOTAL]), following)
        correction = split(identity(1.5) - 0.5 * iterate)
        held = product(under(root, force), correction)
        force = split(held[SAMPLE_TOTAL:])

        shift = product(force, split(top(held)))[:1] / frobenius
        transform = jnp.sqrt((SAMPLE_TOTAL - 1.0) / frobenius) * top(held) + shift
        updated = product(split(transform), (dev_high[q], dev_low[q])) + means[q]
        for v in range(3):
            reply[q, v] = updated[:, v * 128 : (v + 1) * 128].reshape(HALF, 8, 128)

        place = returned.at[turn // 2, turn % 2, :, pl.ds(4 * q, 4), :]

        def source(target, half):
            return reply.at[q, :, target % HALF, pl.ds(4 * half, 4), :]

        def answer(i, carry):
            target = (me + 1 + i) % N_MEM
            for half in range(2):

                @pl.when(target // HALF == half)
                def _():
                    pltpu.make_async_remote_copy(
                        src_ref=source(target, half),
                        dst_ref=place,
                        send_sem=back_send,
                        recv_sem=back_recv,
                        device_id=(band, target),
                        device_id_type=MESH,
                    ).start()

            return carry

        lax.fori_loop(0, N_MEM - 1, answer, 0)
        for half in range(2):

            @pl.when(me // HALF == half)
            def _():
                pltpu.make_async_copy(source(me, half), place, back_recv).start()

    @pl.when(pair < N_MEM - 1)
    def _():
        to_left.wait_recv()

    analyse(1)

    @pl.when(pair > 0)
    def _():
        to_right.wait_recv()

    analyse(0)

    pltpu.make_async_copy(returned, returned, back_recv).wait()

    @pl.when(band < N_BAND - 1)
    def _():
        up.wait_send()

    @pl.when(band > 0)
    def _():
        down.wait_send()

    @pl.when(obs_owner != me)
    def _():
        obs_copy.wait_send()

    @pl.when(pair > 0)
    def _():
        to_left.wait_send()

    @pl.when(pair < N_MEM - 1)
    def _():
        to_right.wait_send()

    most = returned.at[pl.ds(0, HALF - 1)]
    for sem in (fwd_send, back_send):
        pltpu.make_async_copy(most, most, sem).wait()
        rest = returned.at[HALF - 1, 0]
        pltpu.make_async_copy(rest, rest, sem).wait()


def unpack(arrived, out, returned, result, load_sem, store_sem):
    loads = []
    for row in range(ROWS):
        part = pl.ds((row + 3) % 4 * 8, 8)
        loads.append(
            pltpu.make_async_copy(arrived.at[part], returned.at[part], load_sem.at[row])
        )
        loads[-1].start()
    copies = []
    for row in range(ROWS):
        loads[row].wait()
        unpack_row(row, returned, result)
        lanes = pl.ds(row * NLON, NLON)
        for b in range(2):
            copies.append(
                pltpu.make_async_copy(
                    result.at[:, :, pl.ds(4 * b, 4), lanes],
                    out.at[:, :, b, :, lanes],
                    store_sem.at[b, row],
                )
            )
            copies[-1].start()
    for copy in copies:
        copy.wait()


def body(members, diffusivity, observed_site, observed_value, observed_error, observed_count):
    vmem = pl.BlockSpec(memory_space=pltpu.VMEM)
    block = (2, 3, HALF, 8, 128)
    half = (N_MEM // 2, 2, 3, 8, 128)
    state = (3, 2, 8, ROWS * NLON)
    dma = pltpu.SemaphoreType.DMA
    returned = pl.pallas_call(
        kernel,
        out_shape=jax.ShapeDtypeStruct(half, F32),
        in_specs=[
            pl.BlockSpec(memory_space=pl.ANY),
            vmem,
            vmem,
            vmem,
            vmem,
            pl.BlockSpec(memory_space=pltpu.SMEM),
        ],
        out_specs=pl.BlockSpec(memory_space=pl.ANY),
        scratch_shapes=[
            pltpu.VMEM(state, F32),
            pltpu.VMEM((2, 3, 2, 8, NLON), F32),
            pltpu.VMEM(half, F32),
            pltpu.VMEM(block, F32),
            pltpu.VMEM(block, F32),
            pltpu.VMEM((8, SLOTS), F32),
            pltpu.VMEM((8, SLOTS), F32),
            pltpu.VMEM((2, 264, SLOTS), F32),
            pltpu.VMEM((2, 264, SLOTS), F32),
            pltpu.VMEM((2, SAMPLE_TOTAL, STATE), BF16),
            pltpu.VMEM((2, SAMPLE_TOTAL, STATE), BF16),
            pltpu.VMEM((2, 272, STATE), BF16),
            pltpu.VMEM((2, 272, STATE), BF16),
            dma((2,)),
            dma((2,)),
            dma((2,)),
            dma((2,)),
            dma,
            dma((2,)),
            dma((2,)),
            dma((2,)),
            dma,
            dma,
        ],
        compiler_params=pltpu.CompilerParams(
            collective_id=0, has_side_effects=True, vmem_limit_bytes=60 * 2**20
        ),
    )(
        members.transpose(1, 0, 2).reshape(3, 2, 2, 4, ROWS * NLON),
        diffusivity.reshape(1, ROWS * NLON),
        observed_site.reshape(2, SLOTS),
        observed_value.reshape(2, SLOTS),
        observed_error.reshape(2, SLOTS),
        observed_count,
    )
    analysis = pl.pallas_call(
        unpack,
        out_shape=jax.ShapeDtypeStruct((3, 2, 2, 4, ROWS * NLON), F32),
        in_specs=[pl.BlockSpec(memory_space=pl.ANY)],
        out_specs=pl.BlockSpec(memory_space=pl.ANY),
        scratch_shapes=[
            pltpu.VMEM(half, F32),
            pltpu.VMEM(state, F32),
            dma((ROWS,)),
            dma((2, ROWS)),
        ],
        compiler_params=pltpu.CompilerParams(vmem_limit_bytes=60 * 2**20),
    )(returned)
    return analysis.reshape(12, 4, ROWS * NLON).transpose(1, 0, 2)


def solution(mesh):
    in_specs = (
        P("mem", None, "band"),
        P("band"),
        P(("band", "mem")),
        P(("band", "mem")),
        P(("band", "mem")),
        P(("band", "mem")),
    )
    out_specs = P("mem", None, "band")
    return jax.shard_map(body, mesh=mesh, in_specs=in_specs, out_specs=out_specs, check_vma=False)
```

```python
import functools
import math

import jax
import jax.numpy as jnp
from jax import lax
from jax.experimental import pallas as pl
from jax.experimental.pallas import tpu as pltpu
from jax.sharding import PartitionSpec as P

SAMPLE_TOTAL = 256
NLON = 1024
NLAT = 32
N_BAND = 8
N_MEM = 64
HALF = N_MEM // 2
CHIPS_Z = 8
ROWS = NLAT // N_BAND
SLOTS = 128
STATE = 384
CELLS = 32
TRANSPORT_SPEED = 0.5
CORIOLIS = 0.5
MESH = pl.DeviceIdType.MESH
F32 = jnp.float32
BF16 = jnp.bfloat16


def owner_of(turn):
    return turn % HALF * 2 + turn // HALF


def turn_of_pair(pair):
    return (pair + (N_MEM - 16)) % N_MEM


def split(x):
    high = x.astype(BF16)
    return high, (x - high.astype(F32)).astype(BF16)


def product(left, right, transposed=False):
    dims = (((1,), (1,) if transposed else (0,)), ((), ()))
    dot = functools.partial(lax.dot_general, dimension_numbers=dims, preferred_element_type=F32)
    return dot(left[0], right[0]) + (dot(left[0], right[1]) + dot(left[1], right[0]))


def row_coriolis(band, row):
    value = 0.0
    for b in range(N_BAND):
        latitude = math.pi * ((b * ROWS + row + 0.5) / NLAT - 0.5)
        value = jnp.where(band == b, F32(CORIOLIS * math.sin(latitude)), value)
    return value


def stacked(x):
    return jnp.stack([x[:, i * 128 : (i + 1) * 128] for i in range(NLON // 128)])


def lane_of(shape):
    return lax.broadcasted_iota(jnp.int32, shape, len(shape) - 1)


def sublane_of(shape):
    return lax.broadcasted_iota(jnp.int32, shape, len(shape) - 2)


def exchange_halves(x):
    upper = sublane_of(x.shape) >= 4
    odd = lane_of(x.shape) % 64 >= 32
    other = pltpu.roll(x, 4, axis=1)
    moved = jnp.where(upper, pltpu.roll(other, 96, axis=2), pltpu.roll(other, 32, axis=2))
    return jnp.where(upper == odd, x, moved)


def exchange_blocks(first, second):
    low = lane_of(first.shape) < 64
    return (
        jnp.where(low, first, pltpu.roll(second, 64, axis=2)),
        jnp.where(low, pltpu.roll(first, 64, axis=2), second),
    )


def forecast_row(row, band, state, halo_before, halo_after, kappa, packed):
    here = pl.ds(row * NLON, NLON)
    coriolis = row_coriolis(band, row)
    diffusivity = kappa[:, here]
    fresh = []
    for a in range(2):
        center, north, south, east, west = [], [], [], [], []
        for v in range(3):
            x = state[v, a, :, here]
            center.append(x)
            if row + 1 < ROWS:
                north.append(state[v, a, :, pl.ds((row + 1) * NLON, NLON)])
            else:
                north.append(halo_after[v, a])
            if row > 0:
                south.append(state[v, a, :, pl.ds((row - 1) * NLON, NLON)])
            else:
                south.append(halo_before[v, a])
            east.append(pltpu.roll(x, NLON - 1, axis=1))
            west.append(pltpu.roll(x, 1, axis=1))
        diffused = [
            center[v] + diffusivity * (north[v] + south[v] + east[v] + west[v] - 4.0 * center[v])
            for v in range(3)
        ]
        wind_u, wind_v = center[1], center[2]
        thermal = diffused[0] - 0.5 * TRANSPORT_SPEED * (
            wind_u * (east[0] - west[0]) + wind_v * (north[0] - south[0])
        )
        fresh.append((thermal, diffused[1] + coriolis * wind_v, diffused[2] - coriolis * wind_u))
    base = ((row + 3) % 4) * 8
    for v in range(3):
        pair = exchange_blocks(stacked(fresh[0][v]), stacked(fresh[1][v]))
        for p in range(2):
            packed[pl.ds(base, 8), p, v] = exchange_halves(pair[p])


def unpack_row(row, returned, result):
    base = ((row + 3) % 4) * 8
    for v in range(3):
        pair = [exchange_halves(returned[pl.ds(base, 8), p, v]) for p in range(2)]
        for a, x in enumerate(exchange_blocks(*pair)):
            for i in range(8):
                result[v, a, :, pl.ds(row * NLON + i * 128, 128)] = x[i]


def kernel(
    members,
    kappa,
    site,
    value,
    error,
    count,
    returned,
    state,
    halo,
    packed,
    landed,
    reply,
    obs_out,
    obs,
    side_out,
    side_in,
    dev_high,
    dev_low,
    stack_high,
    stack_low,
    load_sem,
    halo_send,
    halo_recv,
    obs_sem,
    fwd_send,
    fwd_recv,
    side_send,
    side_recv,
    back_send,
    back_recv,
):
    band = lax.axis_index("band")
    me = lax.axis_index("mem")
    turn = me % 2 * HALF + me // 2
    pair = (turn + 16) % N_MEM

    loads = [
        pltpu.make_async_copy(
            members.at[:, :, b], state.at[:, :, pl.ds(4 * b, 4), :], load_sem.at[b]
        )
        for b in range(2)
    ]
    for load in loads:
        load.start()

    barrier = pltpu.get_barrier_semaphore()

    def greet(i, carry):
        pl.semaphore_signal(
            barrier, inc=1, device_id=(band, (me + i) % N_MEM), device_id_type=MESH
        )
        return carry

    lax.fori_loop(1, N_MEM, greet, 0)

    @pl.when(band > 0)
    def _():
        pl.semaphore_signal(barrier, inc=1, device_id=(band - 1, me), device_id_type=MESH)

    @pl.when(band < N_BAND - 1)
    def _():
        pl.semaphore_signal(barrier, inc=1, device_id=(band + 1, me), device_id_type=MESH)

    obs_out[0:2, :] = site[...].astype(F32)
    obs_out[2:4, :] = value[...]
    slot = lax.broadcasted_iota(jnp.int32, (1, SLOTS), 1)
    for q in range(2):
        present = (slot < count[q]).astype(F32)
        obs_out[4 + q : 5 + q, :] = present / error[q : q + 1, :]
    obs_out[6:8, :] = jnp.zeros((2, SLOTS), F32)

    @pl.when(band == 0)
    def _():
        halo[0] = jnp.zeros(halo.shape[1:], F32)

    @pl.when(band == N_BAND - 1)
    def _():
        halo[1] = jnp.zeros(halo.shape[1:], F32)

    for load in loads:
        load.wait()
    forecast_row(1, band, state, halo.at[0], halo.at[1], kappa, packed)

    beside = (band > 0).astype(jnp.int32) + (band < N_BAND - 1).astype(jnp.int32)
    pl.semaphore_wait(barrier, N_MEM - 1 + beside)

    up = pltpu.make_async_remote_copy(
        src_ref=state.at[:, :, :, pl.ds((ROWS - 1) * NLON, NLON)],
        dst_ref=halo.at[0],
        send_sem=halo_send.at[0],
        recv_sem=halo_recv.at[0],
        device_id=(jnp.minimum(band + 1, N_BAND - 1), me),
        device_id_type=MESH,
    )
    down = pltpu.make_async_remote_copy(
        src_ref=state.at[:, :, :, pl.ds(0, NLON)],
        dst_ref=halo.at[1],
        send_sem=halo_send.at[1],
        recv_sem=halo_recv.at[1],
        device_id=(jnp.maximum(band - 1, 0), me),
        device_id_type=MESH,
    )

    @pl.when(band < N_BAND - 1)
    def _():
        up.start()

    @pl.when(band > 0)
    def _():
        down.start()

    def dispatch(q, first, number):
        part = pl.ds(4 * q, 4)

        def send_all(half):
            place = landed.at[q, :, me % HALF, pl.ds(4 * half, 4), :]

            def source(there):
                return packed.at[there // 2, there % 2, :, part, :]

            def send(there):
                pltpu.make_async_remote_copy(
                    src_ref=source(there),
                    dst_ref=place,
                    send_sem=fwd_send,
                    recv_sem=fwd_recv.at[q],
                    device_id=(band, owner_of(there)),
                    device_id_type=MESH,
                ).start()

            def one(i, carry):
                send(first + (turn + 1 + i) % number)
                return carry

            lax.fori_loop(0, number - 1, one, 0)
            last = first + turn % number

            @pl.when(last != turn)
            def _():
                send(last)

            @pl.when(last == turn)
            def _():
                pltpu.make_async_copy(source(turn), place, fwd_recv.at[q]).start()

        for half in range(2):

            @pl.when(me // HALF == half)
            def _():
                send_all(half)

    dispatch(0, 0, 16)
    forecast_row(2, band, state, halo.at[0], halo.at[1], kappa, packed)
    dispatch(0, 16, 16)
    dispatch(1, 0, 32)

    obs_owner = owner_of(turn_of_pair(me))
    obs_copy = pltpu.make_async_remote_copy(
        src_ref=obs_out,
        dst_ref=obs,
        send_sem=obs_sem.at[0],
        recv_sem=obs_sem.at[1],
        device_id=(band, obs_owner),
        device_id_type=MESH,
    )

    @pl.when(obs_owner != me)
    def _():
        obs_copy.start()

    @pl.when(obs_owner == me)
    def _():
        pltpu.make_async_copy(obs_out, obs, obs_sem.at[1]).start()

    @pl.when(band > 0)
    def _():
        up.wait_recv()

    @pl.when(band < N_BAND - 1)
    def _():
        down.wait_recv()

    for row in (3, 0):
        forecast_row(row, band, state, halo.at[0], halo.at[1], kappa, packed)
    dispatch(0, 32, 32)

    @pl.when(turn >= HALF)
    def _():
        dispatch(1, 32, 32)

    pltpu.make_async_copy(obs_out, obs, obs_sem.at[1]).wait()
    sites, scales = [], []
    for q in range(2):
        spot = obs[q : q + 1, :].astype(jnp.int32)
        sites.append(spot)
        offset = (spot % CELLS).astype(F32) + 0.5 - 0.5 * CELLS
        inverse = jnp.sqrt(obs[4 + q : 5 + q, :])
        scales.append(
            [
                inverse * jnp.exp(-0.25 * ((offset + shift) / CELLS) ** 2)
                for shift in (0.0, -float(CELLS), float(CELLS))
            ]
        )

    to_left = pltpu.make_async_remote_copy(
        src_ref=side_out.at[0],
        dst_ref=side_in.at[1],
        send_sem=side_send.at[0],
        recv_sem=side_recv.at[1],
        device_id=(band, owner_of(turn_of_pair(jnp.maximum(pair - 1, 0)))),
        device_id_type=MESH,
    )
    to_right = pltpu.make_async_remote_copy(
        src_ref=side_out.at[1],
        dst_ref=side_in.at[0],
        send_sem=side_send.at[1],
        recv_sem=side_recv.at[0],
        device_id=(band, owner_of(turn_of_pair(jnp.minimum(pair + 1, N_MEM - 1)))),
        device_id_type=MESH,
    )

    lead = lax.broadcasted_iota(jnp.int32, (16, SLOTS), 0) == 0
    @pl.when(pair == 0)
    def _():
        side_in[0] = jnp.zeros(side_in.shape[1:], F32)

    @pl.when(pair == N_MEM - 1)
    def _():
        side_in[1] = jnp.zeros(side_in.shape[1:], F32)

    means = []
    for q in range(2):
        pltpu.make_async_copy(landed.at[q], landed.at[q], fwd_recv.at[q]).wait()
        mean = []
        for v in range(3):
            region = landed[q, v].reshape(SAMPLE_TOTAL, 128)
            mean.append(jnp.sum(region, axis=0, keepdims=True) / SAMPLE_TOTAL)
            high, small = split(region - mean[-1])
            dev_high[q, :, pl.ds(v * 128, 128)] = high
            dev_low[q, :, pl.ds(v * 128, 128)] = small
        mean = jnp.concatenate(mean, axis=1)
        means.append(mean)
        entry = lax.broadcasted_iota(jnp.int32, (STATE, SLOTS), 0)
        pick = (entry == sites[q]).astype(F32).astype(BF16)
        perturbed = jnp.dot(dev_high[q], pick, preferred_element_type=F32) + jnp.dot(
            dev_low[q], pick, preferred_element_type=F32
        )
        part = lax.broadcasted_iota(jnp.int32, (16, STATE), 0)
        high = mean.astype(BF16).astype(F32)
        middle = (mean - high).astype(BF16).astype(F32)
        small = mean - high - middle
        parts = jnp.where(
            part == 0, high, jnp.where(part == 1, middle, jnp.where(part == 2, small, 0.0))
        )
        observed_mean = jnp.sum(
            jnp.dot(parts.astype(BF16), pick, preferred_element_type=F32), axis=0, keepdims=True
        )
        innovation = obs[2 + q : 3 + q, :] - observed_mean
        own, rightward, leftward = scales[q]

        def place_slots(region, column, scale):
            lanes = pl.ds(column * SLOTS, SLOTS)
            high, small = split(perturbed * scale)
            stack_high[region, pl.ds(0, SAMPLE_TOTAL), lanes] = high
            stack_low[region, pl.ds(0, SAMPLE_TOTAL), lanes] = small
            high, small = split(jnp.where(lead, innovation * scale, 0.0))
            stack_high[region, pl.ds(SAMPLE_TOTAL, 16), lanes] = high
            stack_low[region, pl.ds(SAMPLE_TOTAL, 16), lanes] = small

        def side_slots(which, scale):
            side_out[which, pl.ds(0, SAMPLE_TOTAL)] = perturbed * scale
            side_out[which, pl.ds(SAMPLE_TOTAL, 8)] = jnp.where(lead[:8], innovation * scale, 0.0)

        if q == 0:
            side_slots(0, leftward)

            @pl.when(pair > 0)
            def _():
                to_left.start()

            place_slots(0, 1, own)
            place_slots(1, 0, rightward)
        else:
            side_slots(1, rightward)

            @pl.when(pair < N_MEM - 1)
            def _():
                to_right.start()

            @pl.when(turn < HALF)
            def _():
                dispatch(1, 32, 32)

            place_slots(1, 1, own)
            place_slots(0, 2, leftward)

    shape = (SAMPLE_TOTAL, SAMPLE_TOTAL)
    diagonal = lax.broadcasted_iota(jnp.int32, shape, 0) == lax.broadcasted_iota(
        jnp.int32, shape, 1
    )

    def identity(scale):
        return jnp.where(diagonal, F32(scale), F32(0.0))

    top = lambda x: x[:SAMPLE_TOTAL]

    def two_steps(x, x_parts):
        square = product(x_parts, x_parts)
        inner = 0.0625 * square - 0.5625 * x + identity(1.6875)
        return product(split(square), split(inner)) + identity(2.25) - 2.4375 * x

    def under(*pieces):
        return tuple(jnp.concatenate(x, axis=0) for x in zip(*pieces))

    def gram_of(q, lanes):
        left = (stack_high[q, :, lanes], stack_low[q, :, lanes])
        return product(left, (top(left[0]), top(left[1])), transposed=True)

    def analyse(q, own_gram):
        lanes = pl.ds(2 * q * SLOTS, SLOTS)
        high, small = split(side_in[q])
        rest = jnp.zeros((8, SLOTS), BF16)
        stack_high[q, pl.ds(0, 272), lanes] = jnp.concatenate([high, rest], axis=0)
        stack_low[q, pl.ds(0, 272), lanes] = jnp.concatenate([small, rest], axis=0)

        gram = own_gram + gram_of(q, lanes)
        force = split(gram[SAMPLE_TOTAL:])
        gram = top(gram) + identity(SAMPLE_TOTAL - 1.0)
        frobenius = jnp.sqrt(
            jnp.sum(jnp.sum(gram * gram, axis=0, keepdims=True), axis=1, keepdims=True)
        )
        scaled = gram / frobenius

        parts = split(scaled)
        root = split(two_steps(scaled, parts))
        held = product(under(parts, force), root)
        force = split(held[SAMPLE_TOTAL:])
        iterate = product(split(top(held)), root)
        parts = split(iterate)
        following = split(two_steps(iterate, parts))
        held = product(under(root, parts, force), following)
        root, force = split(top(held)), split(held[2 * SAMPLE_TOTAL :])
        iterate = product(split(held[SAMPLE_TOTAL : 2 * SAMPLE_TOTAL]), following)
        correction = split(identity(1.5) - 0.5 * iterate)
        held = product(under(root, force), correction)
        force = split(held[SAMPLE_TOTAL:])

        shift = product(force, split(top(held)))[:1] / frobenius
        transform = jnp.sqrt((SAMPLE_TOTAL - 1.0) / frobenius) * top(held) + shift
        updated = product(split(transform), (dev_high[q], dev_low[q])) + means[q]
        for v in range(3):
            reply[q, v] = updated[:, v * 128 : (v + 1) * 128].reshape(HALF, 8, 128)

        place = returned.at[turn // 2, turn % 2, :, pl.ds(4 * q, 4), :]

        def source(target, half):
            return reply.at[q, :, target % HALF, pl.ds(4 * half, 4), :]

        def answer(i, carry):
            target = (me + 1 + i) % N_MEM
            for half in range(2):

                @pl.when(target // HALF == half)
                def _():
                    pltpu.make_async_remote_copy(
                        src_ref=source(target, half),
                        dst_ref=place,
                        send_sem=back_send,
                        recv_sem=back_recv,
                        device_id=(band, target),
                        device_id_type=MESH,
                    ).start()

            return carry

        lax.fori_loop(0, N_MEM - 1, answer, 0)
        for half in range(2):

            @pl.when(me // HALF == half)
            def _():
                pltpu.make_async_copy(source(me, half), place, back_recv).start()

    own_gram = gram_of(1, pl.ds(0, 2 * SLOTS))

    @pl.when(pair < N_MEM - 1)
    def _():
        to_left.wait_recv()

    analyse(1, own_gram)
    own_gram = gram_of(0, pl.ds(SLOTS, 2 * SLOTS))

    @pl.when(pair > 0)
    def _():
        to_right.wait_recv()

    analyse(0, own_gram)

    pltpu.make_async_copy(returned, returned, back_recv).wait()

    @pl.when(band < N_BAND - 1)
    def _():
        up.wait_send()

    @pl.when(band > 0)
    def _():
        down.wait_send()

    @pl.when(obs_owner != me)
    def _():
        obs_copy.wait_send()

    @pl.when(pair > 0)
    def _():
        to_left.wait_send()

    @pl.when(pair < N_MEM - 1)
    def _():
        to_right.wait_send()

    most = returned.at[pl.ds(0, HALF - 1)]
    for sem in (fwd_send, back_send):
        pltpu.make_async_copy(most, most, sem).wait()
        rest = returned.at[HALF - 1, 0]
        pltpu.make_async_copy(rest, rest, sem).wait()


def unpack(arrived, out, returned, result, load_sem, store_sem):
    loads = []
    for row in range(ROWS):
        part = pl.ds((row + 3) % 4 * 8, 8)
        loads.append(
            pltpu.make_async_copy(arrived.at[part], returned.at[part], load_sem.at[row])
        )
        loads[-1].start()
    copies = []
    for row in range(ROWS):
        loads[row].wait()
        unpack_row(row, returned, result)
        lanes = pl.ds(row * NLON, NLON)
        for b in range(2):
            copies.append(
                pltpu.make_async_copy(
                    result.at[:, :, pl.ds(4 * b, 4), lanes],
                    out.at[:, :, b, :, lanes],
                    store_sem.at[b, row],
                )
            )
            copies[-1].start()
    for copy in copies:
        copy.wait()


def body(members, diffusivity, observed_site, observed_value, observed_error, observed_count):
    vmem = pl.BlockSpec(memory_space=pltpu.VMEM)
    block = (2, 3, HALF, 8, 128)
    half = (N_MEM // 2, 2, 3, 8, 128)
    state = (3, 2, 8, ROWS * NLON)
    dma = pltpu.SemaphoreType.DMA
    returned = pl.pallas_call(
        kernel,
        out_shape=jax.ShapeDtypeStruct(half, F32),
        in_specs=[
            pl.BlockSpec(memory_space=pl.ANY),
            vmem,
            vmem,
            vmem,
            vmem,
            pl.BlockSpec(memory_space=pltpu.SMEM),
        ],
        out_specs=pl.BlockSpec(memory_space=pl.ANY),
        scratch_shapes=[
            pltpu.VMEM(state, F32),
            pltpu.VMEM((2, 3, 2, 8, NLON), F32),
            pltpu.VMEM(half, F32),
            pltpu.VMEM(block, F32),
            pltpu.VMEM(block, F32),
            pltpu.VMEM((8, SLOTS), F32),
            pltpu.VMEM((8, SLOTS), F32),
            pltpu.VMEM((2, 264, SLOTS), F32),
            pltpu.VMEM((2, 264, SLOTS), F32),
            pltpu.VMEM((2, SAMPLE_TOTAL, STATE), BF16),
            pltpu.VMEM((2, SAMPLE_TOTAL, STATE), BF16),
            pltpu.VMEM((2, 272, STATE), BF16),
            pltpu.VMEM((2, 272, STATE), BF16),
            dma((2,)),
            dma((2,)),
            dma((2,)),
            dma((2,)),
            dma,
            dma((2,)),
            dma((2,)),
            dma((2,)),
            dma,
            dma,
        ],
        compiler_params=pltpu.CompilerParams(
            collective_id=0, has_side_effects=True, vmem_limit_bytes=60 * 2**20
        ),
    )(
        members.transpose(1, 0, 2).reshape(3, 2, 2, 4, ROWS * NLON),
        diffusivity.reshape(1, ROWS * NLON),
        observed_site.reshape(2, SLOTS),
        observed_value.reshape(2, SLOTS),
        observed_error.reshape(2, SLOTS),
        observed_count,
    )
    analysis = pl.pallas_call(
        unpack,
        out_shape=jax.ShapeDtypeStruct((3, 2, 2, 4, ROWS * NLON), F32),
        in_specs=[pl.BlockSpec(memory_space=pl.ANY)],
        out_specs=pl.BlockSpec(memory_space=pl.ANY),
        scratch_shapes=[
            pltpu.VMEM(half, F32),
            pltpu.VMEM(state, F32),
            dma((ROWS,)),
            dma((2, ROWS)),
        ],
        compiler_params=pltpu.CompilerParams(vmem_limit_bytes=60 * 2**20),
    )(returned)
    return analysis.reshape(12, 4, ROWS * NLON).transpose(1, 0, 2)


def solution(mesh):
    in_specs = (
        P("mem", None, "band"),
        P("band"),
        P(("band", "mem")),
        P(("band", "mem")),
        P(("band", "mem")),
        P(("band", "mem")),
    )
    out_specs = P("mem", None, "band")
    return jax.shard_map(body, mesh=mesh, in_specs=in_specs, out_specs=out_specs, check_vma=False)
```
